256 devices in a mesh: tm: 8 (over z), row: 4 (over x), col: 8 (over y, core).
Axes of the slice: x: 4, y: 4, z: 8, core: 2. Of those that a mesh axis runs over, the one named last changes fastest.
Arguments:
- activations: bfloat16 [32, 64, 128, 256], P('tm', 'row', 'col'), may hold values from -300 to 300
- cotangent: bfloat16 [32, 64, 128, 256], P('tm', 'row', 'col'), may hold values from -80 to 80
- conv_first: bfloat16 [3, 3, 3, 256, 256], replicated, may hold values from -0.078125 to 0.078125
- bias_first: float32 [256], replicated, may hold values from -4 to 4
- gain_first: float32 [256], replicated, may hold values from 0.1 to 1.9
- offset_first: float32 [256], replicated, may hold values from -4 to 4
- conv_second: bfloat16 [3, 3, 3, 256, 256], replicated, may hold values from -0.078125 to 0.078125
- gain_second: float32 [256], replicated, may hold values from 0.1 to 1.9
- offset_second: float32 [256], replicated, may hold values from -4 to 4
Outputs:
- grad_input: bfloat16 [32, 64, 128, 256], P('tm', 'row', 'col')
The draws below stay inside these ranges and needn't reach their ends.
All inputs are finite; a program needn't handle non-finite values.
Results may differ from the reference program's by a relative error of at most 0.0035.
The reference program's roundings to bfloat16 on the way count: a program that leaves them out, or rounds other values in their place, can miss the bound.
Values may be sent and summed in bfloat16 or wider, within the bound.
A program may use at most 64 MiB of HBM per device.

```python
import jax
import jax.numpy as jnp
from jax import lax

C = 256
G = 32
NT = 32
NH = 64
NW = 128


def draw_activations(key, part):
    key = jax.random.fold_in(key, 7)
    key_base, key_channel, key_rough = jax.random.split(key, 3)
    dims = (NT, NH, NW, C)
    base_draw = jnp.clip(jax.random.normal(key_base, dims, jnp.float32), -6.0, 6.0)
    growth = 3.0
    frac_t = jnp.arange(NT, dtype=jnp.float32) / max(NT - 1, 1)
    frac_h = jnp.arange(NH, dtype=jnp.float32) / max(NH - 1, 1)
    frac_w = jnp.arange(NW, dtype=jnp.float32) / max(NW - 1, 1)
    position = growth ** (frac_t[:, None, None, None] + frac_h[None, :, None, None] + frac_w[None, None, :, None] - 1.5)
    channel_scale = 10.0 ** (jax.random.uniform(key_channel, (C,), jnp.float32) - 0.5)
    roughness = jnp.exp(jax.random.uniform(key_rough, dims, jnp.float32, -0.35, 0.35))
    return (base_draw * position * channel_scale * roughness).astype(jnp.bfloat16)


def draw_cotangent(key, part):
    key = jax.random.fold_in(key, 11)
    key_base, key_offset, key_rows, key_cols = jax.random.split(key, 4)
    dims = (NT, NH, NW, C)
    base_draw = jnp.clip(jax.random.normal(key_base, dims, jnp.float32), -6.0, 6.0)
    frac_t = jnp.arange(NT, dtype=jnp.float32) / max(NT - 1, 1)
    channel_offset = jnp.clip(jax.random.normal(key_offset, (C,), jnp.float32), -3.0, 3.0)
    row_scale = 10.0 ** (jax.random.uniform(key_rows, (NH,), jnp.float32) - 0.5)
    col_scale = 10.0 ** (jax.random.uniform(key_cols, (NW,), jnp.float32) - 0.5)
    common = (1.0 + 0.5 * frac_t)[:, None, None, None] * row_scale[None, :, None, None] * col_scale[None, None, :, None] * channel_offset
    return (base_draw + common).astype(jnp.bfloat16)


def gaussian(own_key, shape, spread, reach, kind=jnp.bfloat16):
    values = jax.random.normal(own_key, shape, jnp.float32) * spread
    return jnp.minimum(jnp.maximum(values, -reach), reach).astype(kind)


def setup_inputs(seed: int = 0) -> dict:
    key_of = jax.random.split(jax.random.key(seed), 10)
    activations = draw_activations(jax.random.fold_in(key_of[9], 71), 0)
    cotangent = draw_cotangent(jax.random.fold_in(key_of[9], 71), 0)
    conv_first = gaussian(key_of[2], (3, 3, 3, C, C), (27 * C) ** -0.5, 0.078125)
    bias_first = gaussian(key_of[3], (C,), 1.0, 4.0, jnp.float32)
    gain_first = jnp.clip(1.0 + 0.18 * jax.random.normal(key_of[4], (C,), jnp.float32), 0.1, 1.9)
    offset_first = gaussian(key_of[5], (C,), 1.0, 4.0, jnp.float32)
    conv_second = gaussian(key_of[6], (3, 3, 3, C, C), (27 * C) ** -0.5, 0.078125)
    gain_second = jnp.clip(1.0 + 0.18 * jax.random.normal(key_of[7], (C,), jnp.float32), 0.1, 1.9)
    offset_second = gaussian(key_of[8], (C,), 1.0, 4.0, jnp.float32)
    return dict(activations=activations, cotangent=cotangent, conv_first=conv_first, bias_first=bias_first, gain_first=gain_first, offset_first=offset_first, conv_second=conv_second, gain_second=gain_second, offset_second=offset_second)


eps_norm = 1e-06

def convolve(volume, kernel, padding):
    return lax.conv_general_dilated(volume[None], kernel, (1, 1, 1), padding, dimension_numbers=('NDHWC', 'DHWIO', 'NDHWC'), preferred_element_type=jnp.float32)[0]

def flipped(kernel):
    return jnp.swapaxes(kernel[::-1, ::-1, ::-1], 3, 4)

def frame_counts():
    return ((jnp.arange(NT) + 1).astype(jnp.float32) * float(NH * NW * (C // G)))[:, None]

def moments(prefix, counts):
    group_means = prefix[0] / counts
    squares = prefix[1] / counts
    return (group_means, lax.rsqrt(squares - group_means * group_means + eps_norm))

def grad_terms(totals, group_means, inverse_std, counts):
    first_term = (-inverse_std * totals[0] + totals[1] * inverse_std * inverse_std * group_means) / counts
    second_term = -0.5 * totals[1] * inverse_std * inverse_std / counts
    return jnp.stack([first_term, second_term])

def norm_forward(volume, scale_gain, offset):
    values = volume.astype(jnp.float32).reshape(NT, NH, NW, G, C // G)
    moment_sums = jnp.stack([lax.optimization_barrier(jnp.sum(values, axis=(1, 2, 4))), lax.optimization_barrier(jnp.sum(values * values, axis=(1, 2, 4)))])
    group_means, inverse_std = moments(jnp.cumsum(moment_sums, axis=1), frame_counts())
    normed = (values - group_means[:, None, None, :, None]) * inverse_std[:, None, None, :, None]
    pre_act = normed * scale_gain.reshape(G, C // G) + offset.reshape(G, C // G)
    return (values, group_means, inverse_std, normed, pre_act)

def norm_backward(grad_act, pre_act, normed, values, scale_gain, group_means, inverse_std):
    sigma = jax.nn.sigmoid(pre_act)
    grad_pre = grad_act.reshape(pre_act.shape) * sigma * (1.0 + pre_act * (1.0 - sigma))
    grad_hat = grad_pre * scale_gain.reshape(G, C // G)
    totals = jnp.stack([lax.optimization_barrier(jnp.sum(grad_hat, axis=(1, 2, 4))), lax.optimization_barrier(jnp.sum(grad_hat * normed, axis=(1, 2, 4)))])
    terms = grad_terms(totals, group_means, inverse_std, frame_counts())
    suffix = jnp.flip(jnp.cumsum(jnp.flip(terms, 1), axis=1), 1)
    result = inverse_std[:, None, None, :, None] * grad_hat + suffix[0][:, None, None, :, None] + 2.0 * values * suffix[1][:, None, None, :, None]
    return result.reshape(NT, NH, NW, C)

def reference(activations, cotangent, conv_first, bias_first, gain_first, offset_first, conv_second, gain_second, offset_second):
    values_first, means_first, inverse_first, normed_first, pre_first = norm_forward(activations, gain_first, offset_first)
    active = jax.nn.silu(pre_first).reshape(NT, NH, NW, C).astype(jnp.bfloat16)
    hidden = convolve(active, conv_first, [(2, 0), (1, 1), (1, 1)])
    layer_out = (activations.astype(jnp.float32) + hidden + bias_first).astype(jnp.bfloat16)
    values_second, means_second, inverse_second, normed_second, pre_second = norm_forward(layer_out, gain_second, offset_second)
    grad_second = convolve(cotangent, flipped(conv_second), [(0, 2), (1, 1), (1, 1)])
    grad_mid = (cotangent.astype(jnp.float32) + norm_backward(grad_second, pre_second, normed_second, values_second, gain_second, means_second, inverse_second)).astype(jnp.bfloat16)
    grad_first = convolve(grad_mid, flipped(conv_first), [(0, 2), (1, 1), (1, 1)])
    return (grad_mid.astype(jnp.float32) + norm_backward(grad_first, pre_first, normed_first, values_first, gain_first, means_first, inverse_first)).astype(jnp.bfloat16)
```

```python
import functools
import itertools

import jax
import jax.numpy as jnp
from jax import lax
from jax.experimental import pallas as pl
from jax.experimental.pallas import tpu as pltpu
from jax.sharding import PartitionSpec as P

MESH = pl.DeviceIdType.MESH
BF16, F32 = jnp.bfloat16, jnp.float32
EPS = 1e-6
F, H, W, C, G = 4, 16, 16, 256, 32
TAPS = tuple(itertools.product(range(3), repeat=3))
AXES = ("tm", "row", "col")


def offsets_of(sizes):
    tms, rows, cols = sizes
    plane = [(0, b, d) for b in range(rows) for d in range(cols) if (b, d) != (0, 0)]
    plane.sort(key=lambda o: -(min(o[1], rows - o[1]) + min(o[2], cols - o[2])))
    line = [(a, 0, 0) for a in range(1, tms)]
    rims = [
        (a % tms, b % rows, d % cols)
        for a in (-1, 1)
        for b in (-1, 0, 1)
        for d in (-1, 0, 1)
    ]
    everyone = list(dict.fromkeys(plane + line + rims))
    return plane, line, everyone


def sigmoid(u):
    return 0.5 * jnp.tanh(0.5 * u) + 0.5


def split3(x):
    high = x.astype(BF16)
    rest = x - high.astype(F32)
    middle = rest.astype(BF16)
    low = (rest - middle.astype(F32)).astype(BF16)
    return jnp.concatenate([high, middle, low], axis=0)


def exact_dot(x, picks):
    n = x.shape[0]
    y = jnp.dot(split3(x), picks, preferred_element_type=F32)
    return y[:n] + y[n : 2 * n] + y[2 * n :]


def frame_of_lane(shape):
    return lax.broadcasted_iota(jnp.int32, shape, len(shape) - 1) >> 5


def over_frames(x):
    return x + pltpu.roll(x, 32, 1) + pltpu.roll(x, 64, 1) + pltpu.roll(x, 96, 1)


def running(x):
    f = frame_of_lane(x.shape)
    return (
        x
        + jnp.where(f >= 1, pltpu.roll(x, 32, 1), 0.0)
        + jnp.where(f >= 2, pltpu.roll(x, 64, 1), 0.0)
        + jnp.where(f >= 3, pltpu.roll(x, 96, 1), 0.0)
    )


def running_back(x):
    f = frame_of_lane(x.shape)
    return (
        x
        + jnp.where(f <= 2, pltpu.roll(x, 96, 1), 0.0)
        + jnp.where(f <= 1, pltpu.roll(x, 64, 1), 0.0)
        + jnp.where(f <= 0, pltpu.roll(x, 32, 1), 0.0)
    )


def kernel(
    sizes,
    act_hbm,
    cot_hbm,
    w1_hbm,
    w2_hbm,
    bias1,
    gain1,
    offset1,
    gain2,
    offset2,
    out_ref,
    actf,
    cotf,
    gmf,
    w1,
    w2,
    taps,
    grad,
    lay,
    stage,
    colpack,
    cornerpack,
    colhalo,
    cornerhalo,
    colside,
    part,
    gather_m,
    spread_m,
    stat1,
    stat2,
    ends,
    mine,
    line_mine,
    plane_in,
    line_in,
    in_sem,
    halo_send,
    halo_recv,
    plane_send,
    plane_recv,
    line_send,
    line_recv,
):
    tms, rows, cols = sizes
    t, r, c = (lax.axis_index(a) for a in AXES)
    plane, line, everyone = offsets_of(sizes)
    plane_cells = float(H * rows * W * cols * (C // G))

    def at(o):
        return (
            lax.rem(t + (o[0] % tms), tms),
            lax.rem(r + (o[1] % rows), rows),
            lax.rem(c + (o[2] % cols), cols),
        )

    barrier = pltpu.get_barrier_semaphore()
    for o in everyone:
        pl.semaphore_signal(barrier, inc=1, device_id=at(o), device_id_type=MESH)

    loads = [
        pltpu.make_async_copy(act_hbm, actf.at[pl.ds(2, F), pl.ds(1, H)], in_sem.at[0]),
        pltpu.make_async_copy(cot_hbm, cotf.at[pl.ds(0, F), pl.ds(1, H)], in_sem.at[1]),
        pltpu.make_async_copy(w1_hbm, w1, in_sem.at[2]),
        pltpu.make_async_copy(w2_hbm, w2, in_sem.at[3]),
    ]
    for load in loads:
        load.start()

    channel = lax.broadcasted_iota(jnp.int32, (C, 128), 0) >> 3
    group = lax.broadcasted_iota(jnp.int32, (C, 128), 1) & (G - 1)
    gather_m[...] = jnp.where(channel == group, 1.0, 0.0).astype(BF16)
    channel = lax.broadcasted_iota(jnp.int32, (128, C), 1) >> 3
    group = lax.broadcasted_iota(jnp.int32, (128, C), 0) & (G - 1)
    spread_m[...] = jnp.where(channel == group, 1.0, 0.0).astype(BF16)

    def packed_sums():
        y = exact_dot(part[...].reshape(2 * F * 8, C), gather_m[...])
        y = y.reshape(2, F, 8, 128)
        f = frame_of_lane((2, 8, 128))
        z = jnp.zeros((2, 8, 128), F32)
        for i in range(F):
            z = z + jnp.where(f == i, y[:, i], 0.0)
        return jnp.sum(z, axis=1)

    def plane_copy(k, j):
        return pltpu.make_async_remote_copy(
            src_ref=mine.at[k],
            dst_ref=plane_in.at[k, j],
            send_sem=plane_send.at[k],
            recv_sem=plane_recv.at[k],
            device_id=at(plane[j]),
            device_id_type=MESH,
        )

    def line_copy(k, j):
        return pltpu.make_async_remote_copy(
            src_ref=line_mine.at[k],
            dst_ref=line_in.at[k, j],
            send_sem=line_send.at[k],
            recv_sem=line_recv.at[k],
            device_id=at(line[j]),
            device_id_type=MESH,
        )

    def await_all(buffer, sem):
        pltpu.make_async_copy(buffer, buffer, sem).wait()

    def plane_start(k):
        mine[k] = packed_sums()
        for j in range(len(plane)):
            plane_copy(k, j).start()

    def plane_end(k):
        await_all(plane_in.at[k], plane_recv.at[k])
        return mine[k] + jnp.sum(plane_in[k], axis=0)

    def line_start(k, value):
        line_mine[k] = value
        for j in range(len(line)):
            line_copy(k, j).start()

    def line_end(k):
        await_all(line_in.at[k], line_recv.at[k])
        return [line_in[k, j] for j in range(len(line))]

    def counts(first_frame):
        f = first_frame + frame_of_lane((1, 128)) + 1
        return jnp.maximum(f, 1).astype(F32) * plane_cells

    def moments(prefix, n):
        mean = prefix[0:1] / n
        return mean, lax.rsqrt(prefix[1:2] / n - mean * mean + EPS)

    def spread(first, second, before=None):
        row = lax.broadcasted_iota(jnp.int32, (8, 128), 0)
        f = frame_of_lane((8, 128))
        halves = []
        for i, own in enumerate((first, second)):
            own = jnp.broadcast_to(own, (8, 128))
            if before is None:
                halves.append(jnp.where(f == row, own, 0.0))
            else:
                ahead = jnp.broadcast_to(before[i], (8, 128))
                frame = jnp.where(row < 2, row + 2, row - 2)
                halves.append(jnp.where(f == frame, jnp.where(row < 2, ahead, own), 0.0))
        return exact_dot(jnp.concatenate(halves, axis=0), spread_m[...])

    def forward_end(k, layer):
        got = line_end(k)
        zero = jnp.zeros((2, 128), F32)
        near = jnp.where(t >= 1, got[0], zero)
        far = zero
        for j in range(1, len(line)):
            far = far + jnp.where(t >= j + 1, got[j], zero)
        own = moments(over_frames(far + near) + running(line_mine[k]), counts(t * F))
        ends[layer, 0:1] = own[0]
        ends[layer, 1:2] = own[1]
        before = None
        if layer == 0:
            before = moments(over_frames(far) + running(near), counts(t * F - F))
        return spread(own[0], own[1], before)

    def backward_terms(k, layer):
        totals = plane_end(k)
        mean, inverse = ends[layer, 0:1], ends[layer, 1:2]
        n = counts(t * F)
        a, b = totals[0:1], totals[1:2]
        first = (-inverse * a + b * inverse * inverse * mean) / n
        second = -0.5 * b * inverse * inverse / n
        return jnp.concatenate([first, second], axis=0)

    def backward_end(k):
        got = line_end(k)
        zero = jnp.zeros((2, 128), F32)
        later = zero
        for j in range(len(line)):
            later = later + jnp.where(t < j + 1, got[j], zero)
        rest = over_frames(later) + running_back(line_mine[k])
        return spread(rest[0:1], rest[1:2])

    def put_stage(start, x):
        for i in range(2):
            stage[i, pl.ds(start, x.shape[0])] = x[:, i * 128 : i * 128 + 128]

    def staged(start, size, stride):
        return jnp.concatenate(
            [stage[i, pl.ds(start, size, stride=stride), :] for i in range(2)], axis=1
        )

    def pack_rims(k):
        for side, column in enumerate((0, W - 1)):
            for f in range(F):
                rim = staged(f * H * W + column, H, W)
                colpack[k, side, f] = rim.astype(BF16)
            for end, line_at in enumerate((0, H - 1)):
                cornerpack[k, end, side] = staged(line_at * W + column, F, H * W)

    def rim_copies(k, full, own, halo, turn):
        last = own + (F - 2 if turn > 0 else 0)
        inner = F - 2 if turn > 0 else 0
        moves = [((turn, 0, 0), full.at[pl.ds(last, 2), pl.ds(1, H)], full.at[pl.ds(halo, 2), pl.ds(1, H)])]
        for step, src, dst in ((1, H, 0), (-1, 1, H + 1)):
            moves.append(((0, step, 0), full.at[pl.ds(own, F), src], full.at[pl.ds(own, F), dst]))
            moves.append(((turn, step, 0), full.at[pl.ds(last, 2), src], full.at[pl.ds(halo, 2), dst]))
        for step, src, dst in ((1, 1, 0), (-1, 0, 1)):
            moves.append(((0, 0, step), colpack.at[k, src], colhalo.at[k, dst, pl.ds(own, F)]))
            moves.append(
                ((turn, 0, step), colpack.at[k, src, pl.ds(inner, 2)], colhalo.at[k, dst, pl.ds(halo, 2)])
            )
        for down, over in itertools.product((1, -1), repeat=2):
            src = cornerpack.at[k, int(down > 0), int(over > 0)]
            place = (int(down < 0), int(over < 0))
            moves.append(((0, down, over), src, cornerhalo.at[k, 0, place[0], place[1]]))
            moves.append(((turn, down, over), src, cornerhalo.at[k, 1, place[0], place[1]]))
        return [
            pltpu.make_async_remote_copy(
                src_ref=src,
                dst_ref=dst,
                send_sem=halo_send.at[k, j],
                recv_sem=halo_recv.at[k, j],
                device_id=at(o),
                device_id_type=MESH,
            )
            for j, (o, src, dst) in enumerate(moves)
        ]

    def side_columns(k, own, halo, turn, change):
        inner = F - 2 if turn > 0 else 0
        for side in range(2):

            def one(f, carry, side=side):
                colside[side, f, pl.ds(1, H)] = change(colhalo[k, side, f].astype(F32), f)
                return carry

            lax.fori_loop(0, F + 2, one, 0)
            for end, place in ((0, 0), (1, H + 1)):
                for f in range(F):
                    value = cornerhalo[k, 0, end, side, pl.ds(f, 1)]
                    colside[side, own + f, pl.ds(place, 1)] = change(value, own + f)
                for f in range(2):
                    value = cornerhalo[k, 1, end, side, pl.ds(inner + f, 1)]
                    colside[side, halo + f, pl.ds(place, 1)] = change(value, halo + f)

        @pl.when(c == 0)
        def _():
            colside[0] = jnp.zeros(colside.shape[1:], F32)

        @pl.when(c == cols - 1)
        def _():
            colside[1] = jnp.zeros(colside.shape[1:], F32)

    def build(full, halo, edge, change):
        column = lax.broadcasted_iota(jnp.int32, (6, W, C), 1)

        def one(f, carry):
            for h in range(0, H + 2, 6):
                x = change(full[f, pl.ds(h, 6)].astype(F32), f)
                left = colside[0, f, pl.ds(h, 6)].reshape(6, 1, C)
                right = colside[1, f, pl.ds(h, 6)].reshape(6, 1, C)
                taps[1, f, pl.ds(h, 6)] = x.astype(BF16)
                taps[0, f, pl.ds(h, 6)] = jnp.where(
                    column == 0, left, pltpu.roll(x, 1, 1)
                ).astype(BF16)
                taps[2, f, pl.ds(h, 6)] = jnp.where(
                    column == W - 1, right, pltpu.roll(x, W - 1, 1)
                ).astype(BF16)
            return carry

        lax.fori_loop(0, F + 2, one, 0)

        @pl.when(r == 0)
        def _():
            taps[:, :, 0] = jnp.zeros((3, F + 2, W, C), BF16)

        @pl.when(r == rows - 1)
        def _():
            taps[:, :, H + 1] = jnp.zeros((3, F + 2, W, C), BF16)

        @pl.when(t == edge)
        def _():
            for f in range(2):
                for dw in range(3):
                    taps[dw, halo + f] = jnp.zeros((H + 2, W, C), BF16)

    def convolve(f, weights, back):
        left = jnp.concatenate(
            [
                taps[dw, pl.ds(f + dt, 2), pl.ds(dh, H)].reshape(2 * H * W, C)
                for dt, dh, dw in TAPS
            ],
            axis=1,
        )
        if back:
            right = jnp.concatenate([weights[26 - n] for n in range(27)], axis=1)
            return lax.dot_general(left, right, (((1,), (1,)), ((), ())), preferred_element_type=F32)
        return jnp.dot(left, weights[...].reshape(27 * C, C), preferred_element_type=F32)

    def row_of(ref, i):
        return ref[pl.ds(i, 1), :]

    def sums(x):
        return jnp.sum(x.reshape(-1, 8, C), axis=0)

    def norm_grad(values, d, mean, inverse, gain, offset):
        normed = (values - mean) * inverse
        pre = normed * gain + offset
        s = sigmoid(pre)
        e = d * s * (1.0 + pre * (1.0 - s)) * gain
        return e, sums(e), sums(e * normed)

    vectors = [ref[...].reshape(1, C) for ref in (bias1, gain1, offset1, gain2, offset2)]
    bias1, gain1, offset1, gain2, offset2 = vectors

    loads[0].wait()

    def first_sums(f, carry):
        x = actf[f + 2, pl.ds(1, H)].astype(F32).reshape(H * W, C)
        put_stage(f * H * W, x)
        part[0, f] = sums(x)
        part[1, f] = sums(x * x)
        return carry

    lax.fori_loop(0, F, first_sums, 0)
    pack_rims(0)
    pl.semaphore_wait(barrier, len(everyone))
    plane_start(0)
    past = rim_copies(0, actf, 2, 0, 1)
    for copy in past:
        copy.start()
    loads[1].wait()

    def to_stage(f, carry):
        put_stage(f * H * W, cotf[f, pl.ds(1, H)].astype(F32).reshape(H * W, C))
        return carry

    lax.fori_loop(0, F, to_stage, 0)
    pack_rims(1)
    future = rim_copies(1, cotf, 0, 4, -1)
    for copy in future:
        copy.start()
    line_start(0, plane_end(0))
    stat1[...] = forward_end(0, 0)

    for copy in past:
        copy.wait_recv()

    def activate(x, f):
        shape = (1,) * (x.ndim - 1) + (C,)
        mean = row_of(stat1, f).reshape(shape)
        inverse = row_of(stat1, f + 8).reshape(shape)
        u = (x - mean) * inverse * gain1.reshape(shape) + offset1.reshape(shape)
        return u * sigmoid(u)

    side_columns(0, 2, 0, 1, activate)
    build(actf, 0, 0, activate)
    loads[2].wait()

    def first_layer(i, carry):
        f = 2 * i
        hidden = convolve(f, w1, False)
        x = actf[pl.ds(f + 2, 2), pl.ds(1, H)].astype(F32).reshape(2 * H * W, C)
        y = (x + hidden + bias1).astype(BF16)
        lay[pl.ds(f, 2)] = y.reshape(2, H, W, C)
        y = y.astype(F32)
        for j in range(2):
            z = y[j * H * W : (j + 1) * H * W]
            part[0, f + j] = sums(z)
            part[1, f + j] = sums(z * z)
        return carry

    lax.fori_loop(0, F // 2, first_layer, 0)
    plane_start(1)

    for copy in future:
        copy.wait_recv()
    loads[3].wait()
    same = lambda x, f: x
    side_columns(1, 0, 4, -1, same)
    build(cotf, 4, tms - 1, same)

    def second_grad(f):
        grad[pl.ds(f, 2)] = convolve(f, w2, True).reshape(2, H, W, C)

    second_grad(0)
    line_start(1, plane_end(1))
    second_grad(2)
    stat2[...] = forward_end(1, 1)

    def second_norm(f, carry):
        mean, inverse = row_of(stat2, f), row_of(stat2, f + 8)
        a = b = jnp.zeros((8, C), F32)
        for h in range(0, H, 8):
            v = lay[f, pl.ds(h, 8)].astype(F32).reshape(8 * W, C)
            d = grad[f, pl.ds(h, 8)].reshape(8 * W, C)
            e, da, db = norm_grad(v, d, mean, inverse, gain2, offset2)
            grad[f, pl.ds(h, 8)] = e.reshape(8, W, C)
            a, b = a + da, b + db
        part[0, f] = a
        part[1, f] = b
        return carry

    lax.fori_loop(0, F, second_norm, 0)
    plane_start(2)
    line_start(2, backward_terms(2, 1))
    rest2 = backward_end(2)
    ends_rows = stat2[8:16]
    stat2[0:8] = ends_rows
    part[0, 0] = rest2[0:8]
    part[0, 1] = rest2[8:16]

    def middle(f, carry):
        inverse = row_of(stat2, f)
        r1 = part[0, 0, pl.ds(f, 1)]
        r2 = part[0, 1, pl.ds(f, 1)]
        for h in range(0, H, 8):
            v = lay[f, pl.ds(h, 8)].astype(F32).reshape(8 * W, C)
            e = grad[f, pl.ds(h, 8)].reshape(8 * W, C)
            x = cotf[f, pl.ds(h + 1, 8)].astype(F32).reshape(8 * W, C)
            y = (x + (inverse * e + r1 + 2.0 * v * r2)).astype(BF16)
            gmf[f, pl.ds(h + 1, 8)] = y.reshape(8, W, C)
            put_stage(f * H * W + h * W, y.astype(F32))
        return carry

    lax.fori_loop(0, F, middle, 0)
    pack_rims(2)
    middle_rims = rim_copies(2, gmf, 0, 4, -1)
    for copy in middle_rims:
        copy.start()
    for copy in middle_rims:
        copy.wait_recv()

    side_columns(2, 0, 4, -1, same)
    build(gmf, 4, tms - 1, same)

    def first_grad(i, carry):
        f = 2 * i
        grad[pl.ds(f, 2)] = convolve(f, w1, True).reshape(2, H, W, C)
        return carry

    lax.fori_loop(0, F // 2, first_grad, 0)

    def first_norm(f, carry):
        mean, inverse = row_of(stat1, f + 2), row_of(stat1, f + 10)
        a = b = jnp.zeros((8, C), F32)
        for h in range(0, H, 8):
            v = actf[f + 2, pl.ds(h + 1, 8)].astype(F32).reshape(8 * W, C)
            d = grad[f, pl.ds(h, 8)].reshape(8 * W, C)
            e, da, db = norm_grad(v, d, mean, inverse, gain1, offset1)
            grad[f, pl.ds(h, 8)] = e.reshape(8, W, C)
            a, b = a + da, b + db
        part[0, f] = a
        part[1, f] = b
        return carry

    lax.fori_loop(0, F, first_norm, 0)
    plane_start(3)
    line_start(3, backward_terms(3, 0))
    rest1 = backward_end(3)
    part[0, 0] = rest1[0:8]
    part[0, 1] = rest1[8:16]

    def finish(f, carry):
        inverse = row_of(stat1, f + 10)
        r1 = part[0, 0, pl.ds(f, 1)]
        r2 = part[0, 1, pl.ds(f, 1)]
        for h in range(0, H, 8):
            v = actf[f + 2, pl.ds(h + 1, 8)].astype(F32).reshape(8 * W, C)
            e = grad[f, pl.ds(h, 8)].reshape(8 * W, C)
            x = gmf[f, pl.ds(h + 1, 8)].astype(F32).reshape(8 * W, C)
            y = x + (inverse * e + r1 + 2.0 * v * r2)
            out_ref[f, pl.ds(h, 8)] = y.astype(BF16).reshape(8, W, C)
        return carry

    lax.fori_loop(0, F, finish, 0)

    for copy in past + future + middle_rims:
        copy.wait_send()
    for k in range(4):
        await_all(plane_in.at[k], plane_send.at[k])
        await_all(line_in.at[k], line_send.at[k])


def solution(mesh):
    sizes = tuple(mesh.shape[a] for a in AXES)
    n_plane, n_line = sizes[1] * sizes[2] - 1, sizes[0] - 1
    rims = 17
    full = (F + 2, H + 2, W, C)

    def step(act, cot, w1, b1, g1, o1, w2, g2, o2):
        hbm = pl.BlockSpec(memory_space=pl.ANY)
        vmem = pl.BlockSpec(memory_space=pltpu.VMEM)
        return pl.pallas_call(
            functools.partial(kernel, sizes),
            name="vae_grad",
            out_shape=jax.ShapeDtypeStruct((F, H, W, C), BF16),
            in_specs=[hbm] * 4 + [vmem] * 5,
            out_specs=vmem,
            scratch_shapes=[
                pltpu.VMEM(full, BF16),
                pltpu.VMEM(full, BF16),
                pltpu.VMEM(full, BF16),
                pltpu.VMEM((27, C, C), BF16),
                pltpu.VMEM((27, C, C), BF16),
                pltpu.VMEM((3,) + full, BF16),
                pltpu.VMEM((F, H, W, C), F32),
                pltpu.VMEM((F, H, W, C), BF16),
                pltpu.VMEM((2, F * H * W, 128), F32),
                pltpu.VMEM((3, 2, F, H, C), BF16),
                pltpu.VMEM((3, 2, 2, F, C), F32),
                pltpu.VMEM((3, 2, F + 2, H, C), BF16),
                pltpu.VMEM((3, 2, 2, 2, F, C), F32),
                pltpu.VMEM((2, F + 2, 24, C), F32),
                pltpu.VMEM((2, F, 8, C), F32),
                pltpu.VMEM((C, 128), BF16),
                pltpu.VMEM((128, C), BF16),
                pltpu.VMEM((16, C), F32),
                pltpu.VMEM((16, C), F32),
                pltpu.VMEM((2, 2, 128), F32),
                pltpu.VMEM((4, 2, 128), F32),
                pltpu.VMEM((4, 2, 128), F32),
                pltpu.VMEM((4, n_plane, 2, 128), F32),
                pltpu.VMEM((4, n_line, 2, 128), F32),
                pltpu.SemaphoreType.DMA((4,)),
                pltpu.SemaphoreType.DMA((3, rims)),
                pltpu.SemaphoreType.DMA((3, rims)),
                pltpu.SemaphoreType.DMA((4,)),
                pltpu.SemaphoreType.DMA((4,)),
                pltpu.SemaphoreType.DMA((4,)),
                pltpu.SemaphoreType.DMA((4,)),
            ],
            compiler_params=pltpu.CompilerParams(
                collective_id=0, has_side_effects=True, vmem_limit_bytes=48 << 20
            ),
        )(act, cot, w1.reshape(27, C, C), w2.reshape(27, C, C), b1, g1, o1, g2, o2)

    tile = P(*AXES, None)
    return jax.shard_map(
        step,
        mesh=mesh,
        in_specs=(tile, tile) + (P(),) * 7,
        out_specs=tile,
        check_vma=False,
    )
```

```python
import functools
import itertools

import jax
import jax.numpy as jnp
from jax import lax
from jax.experimental import pallas as pl
from jax.experimental.pallas import tpu as pltpu
from jax.sharding import PartitionSpec as P

MESH = pl.DeviceIdType.MESH
BF16, F32 = jnp.bfloat16, jnp.float32
EPS = 1e-6
F, H, W, C, G = 4, 16, 16, 256, 32
TAPS = tuple(itertools.product(range(3), repeat=3))
AXES = ("tm", "row", "col")


def offsets_of(sizes):
    tms, rows, cols = sizes
    plane = [(0, b, d) for b in range(rows) for d in range(cols) if (b, d) != (0, 0)]
    plane.sort(key=lambda o: -(min(o[1], rows - o[1]) + min(o[2], cols - o[2])))
    line = [(a, 0, 0) for a in range(1, tms)]
    rims = [
        (a % tms, b % rows, d % cols)
        for a in (-1, 1)
        for b in (-1, 0, 1)
        for d in (-1, 0, 1)
    ]
    everyone = list(dict.fromkeys(plane + line + rims))
    return plane, line, everyone


def sigmoid(u):
    return 0.5 * jnp.tanh(0.5 * u) + 0.5


def split3(x):
    high = x.astype(BF16)
    rest = x - high.astype(F32)
    middle = rest.astype(BF16)
    low = (rest - middle.astype(F32)).astype(BF16)
    return jnp.concatenate([high, middle, low], axis=0)


def exact_dot(x, picks):
    n = x.shape[0]
    y = jnp.dot(split3(x), picks, preferred_element_type=F32)
    return y[:n] + y[n : 2 * n] + y[2 * n :]


def frame_of_lane(shape):
    return lax.broadcasted_iota(jnp.int32, shape, len(shape) - 1) >> 5


def over_frames(x):
    return x + pltpu.roll(x, 32, 1) + pltpu.roll(x, 64, 1) + pltpu.roll(x, 96, 1)


def running(x):
    f = frame_of_lane(x.shape)
    return (
        x
        + jnp.where(f >= 1, pltpu.roll(x, 32, 1), 0.0)
        + jnp.where(f >= 2, pltpu.roll(x, 64, 1), 0.0)
        + jnp.where(f >= 3, pltpu.roll(x, 96, 1), 0.0)
    )


def running_back(x):
    f = frame_of_lane(x.shape)
    return (
        x
        + jnp.where(f <= 2, pltpu.roll(x, 96, 1), 0.0)
        + jnp.where(f <= 1, pltpu.roll(x, 64, 1), 0.0)
        + jnp.where(f <= 0, pltpu.roll(x, 32, 1), 0.0)
    )


def kernel(
    sizes,
    act_hbm,
    cot_hbm,
    w1_hbm,
    w2_hbm,
    bias1_hbm,
    gain1_hbm,
    offset1_hbm,
    gain2_hbm,
    offset2_hbm,
    out_ref,
    actf,
    cotf,
    gmf,
    w1,
    w2,
    bias1,
    gain1,
    offset1,
    gain2,
    offset2,
    taps,
    grad,
    layf,
    xf,
    stage,
    colpack,
    cornerpack,
    colhalo,
    cornerhalo,
    colside,
    part,
    gather_m,
    spread_m,
    stat1,
    stat2,
    rest1,
    rest2,
    ends,
    mine,
    line_mine,
    plane_in,
    line_in,
    in_sem,
    halo_send,
    halo_recv,
    plane_send,
    plane_recv,
    line_send,
    line_recv,
):
    tms, rows, cols = sizes
    t, r, c = (lax.axis_index(a) for a in AXES)
    plane, line, everyone = offsets_of(sizes)
    plane_cells = float(H * rows * W * cols * (C // G))

    def at(o):
        return (
            lax.rem(t + (o[0] % tms), tms),
            lax.rem(r + (o[1] % rows), rows),
            lax.rem(c + (o[2] % cols), cols),
        )

    barrier = pltpu.get_barrier_semaphore()
    for o in everyone:
        pl.semaphore_signal(barrier, inc=1, device_id=at(o), device_id_type=MESH)

    loads = [
        pltpu.make_async_copy(act_hbm, actf.at[pl.ds(2, F), pl.ds(1, H)], in_sem.at[0]),
        pltpu.make_async_copy(cot_hbm, cotf.at[pl.ds(0, F), pl.ds(1, H)], in_sem.at[1]),
        pltpu.make_async_copy(w1_hbm, w1, in_sem.at[2]),
        pltpu.make_async_copy(w2_hbm, w2, in_sem.at[3]),
        pltpu.make_async_copy(bias1_hbm, bias1, in_sem.at[4]),
        pltpu.make_async_copy(gain1_hbm, gain1, in_sem.at[5]),
        pltpu.make_async_copy(offset1_hbm, offset1, in_sem.at[6]),
        pltpu.make_async_copy(gain2_hbm, gain2, in_sem.at[7]),
        pltpu.make_async_copy(offset2_hbm, offset2, in_sem.at[8]),
    ]
    for load in loads:
        load.start()

    channel = lax.broadcasted_iota(jnp.int32, (C, 128), 0) >> 3
    group = lax.broadcasted_iota(jnp.int32, (C, 128), 1) & (G - 1)
    gather_m[...] = jnp.where(channel == group, 1.0, 0.0).astype(BF16)
    channel = lax.broadcasted_iota(jnp.int32, (128, C), 1) >> 3
    group = lax.broadcasted_iota(jnp.int32, (128, C), 0) & (G - 1)
    spread_m[...] = jnp.where(channel == group, 1.0, 0.0).astype(BF16)

    def packed_sums():
        y = exact_dot(part[...].reshape(2 * F * 8, C), gather_m[...])
        y = y.reshape(2, F, 8, 128)
        f = frame_of_lane((2, 8, 128))
        z = jnp.zeros((2, 8, 128), F32)
        for i in range(F):
            z = z + jnp.where(f == i, y[:, i], 0.0)
        return jnp.sum(z, axis=1)

    def plane_copy(k, j):
        return pltpu.make_async_remote_copy(
            src_ref=mine.at[k],
            dst_ref=plane_in.at[k, j],
            send_sem=plane_send.at[k],
            recv_sem=plane_recv.at[k],
            device_id=at(plane[j]),
            device_id_type=MESH,
        )

    def line_copy(k, j):
        return pltpu.make_async_remote_copy(
            src_ref=line_mine.at[k],
            dst_ref=line_in.at[k, j],
            send_sem=line_send.at[k],
            recv_sem=line_recv.at[k],
            device_id=at(line[j]),
            device_id_type=MESH,
        )

    def await_all(buffer, sem):
        pltpu.make_async_copy(buffer, buffer, sem).wait()

    def plane_start(k):
        mine[k] = packed_sums()
        for j in range(len(plane)):
            plane_copy(k, j).start()

    def plane_end(k):
        await_all(plane_in.at[k], plane_recv.at[k])
        return mine[k] + jnp.sum(plane_in[k], axis=0)

    def line_start(k, value):
        line_mine[k] = value
        for j in range(len(line)):
            line_copy(k, j).start()

    def line_end(k):
        await_all(line_in.at[k], line_recv.at[k])
        return [line_in[k, j] for j in range(len(line))]

    def counts(first_frame):
        f = first_frame + frame_of_lane((1, 128)) + 1
        return jnp.maximum(f, 1).astype(F32) * plane_cells

    def moments(prefix, n):
        mean = prefix[0:1] / n
        return mean, lax.rsqrt(prefix[1:2] / n - mean * mean + EPS)

    def spread(first, second, before=None, after=None):
        row = lax.broadcasted_iota(jnp.int32, (8, 128), 0)
        f = frame_of_lane((8, 128))
        halves = []
        for i, own in enumerate((first, second)):
            own = jnp.broadcast_to(own, (8, 128))
            if before is not None:
                ahead = jnp.broadcast_to(before[i], (8, 128))
                frame = jnp.where(row < 2, row + 2, row - 2)
                own = jnp.where(row < 2, ahead, own)
            elif after is not None:
                behind = jnp.broadcast_to(after[i], (8, 128))
                frame = jnp.where(row < F, row, row - F)
                own = jnp.where(row < F, own, behind)
            else:
                frame = row
            halves.append(jnp.where(f == frame, own, 0.0))
        return exact_dot(jnp.concatenate(halves, axis=0), spread_m[...])

    def forward_end(k, layer):
        got = line_end(k)
        zero = jnp.zeros((2, 128), F32)
        near = jnp.where(t >= 1, got[0], zero)
        far = zero
        for j in range(1, len(line)):
            far = far + jnp.where(t >= j + 1, got[j], zero)
        own = moments(over_frames(far + near) + running(line_mine[k]), counts(t * F))
        ends[layer, 0:1] = own[0]
        ends[layer, 1:2] = own[1]
        before = None
        if layer == 0:
            before = moments(over_frames(far) + running(near), counts(t * F - F))
        return spread(own[0], own[1], before)

    def backward_terms(k, layer):
        totals = plane_end(k)
        mean, inverse = ends[layer, 0:1], ends[layer, 1:2]
        n = counts(t * F)
        a, b = totals[0:1], totals[1:2]
        first = (-inverse * a + b * inverse * inverse * mean) / n
        second = -0.5 * b * inverse * inverse / n
        return jnp.concatenate([first, second], axis=0)

    def backward_end(k):
        got = line_end(k)
        zero = jnp.zeros((2, 128), F32)
        near = jnp.where(t < tms - 1, got[-1], zero)
        far = zero
        for j in range(len(line) - 1):
            far = far + jnp.where(t < j + 1, got[j], zero)
        rest = over_frames(far + near) + running_back(line_mine[k])
        behind = over_frames(far) + running_back(near)
        return spread(rest[0:1], rest[1:2], after=(behind[0:1], behind[1:2]))

    def put_stage(start, x):
        for i in range(2):
            stage[i, pl.ds(start, x.shape[0])] = x[:, i * 128 : i * 128 + 128]

    def staged(start, size, stride):
        return jnp.concatenate(
            [stage[i, pl.ds(start, size, stride=stride), :] for i in range(2)], axis=1
        )

    def pack_rims(k):
        for side, column in enumerate((0, W - 1)):
            for f in range(F):
                rim = staged(f * H * W + column, H, W)
                colpack[k, side, f] = rim.astype(BF16)
            for end, line_at in enumerate((0, H - 1)):
                cornerpack[k, end, side] = staged(line_at * W + column, F, H * W)

    def rim_copies(k, full, own, halo, turn):
        last = own + (F - 2 if turn > 0 else 0)
        inner = F - 2 if turn > 0 else 0
        moves = [((turn, 0, 0), full.at[pl.ds(last, 2), pl.ds(1, H)], full.at[pl.ds(halo, 2), pl.ds(1, H)])]
        for step, src, dst in ((1, H, 0), (-1, 1, H + 1)):
            moves.append(((0, step, 0), full.at[pl.ds(own, F), src], full.at[pl.ds(own, F), dst]))
            moves.append(((turn, step, 0), full.at[pl.ds(last, 2), src], full.at[pl.ds(halo, 2), dst]))
        for step, src, dst in ((1, 1, 0), (-1, 0, 1)):
            moves.append(((0, 0, step), colpack.at[k, src], colhalo.at[k, dst, pl.ds(own, F)]))
            moves.append(
                ((turn, 0, step), colpack.at[k, src, pl.ds(inner, 2)], colhalo.at[k, dst, pl.ds(halo, 2)])
            )
        for down, over in itertools.product((1, -1), repeat=2):
            src = cornerpack.at[k, int(down > 0), int(over > 0)]
            place = (int(down < 0), int(over < 0))
            moves.append(((0, down, over), src, cornerhalo.at[k, 0, place[0], place[1]]))
            moves.append(((turn, down, over), src, cornerhalo.at[k, 1, place[0], place[1]]))
        return [
            pltpu.make_async_remote_copy(
                src_ref=src,
                dst_ref=dst,
                send_sem=halo_send.at[k, j],
                recv_sem=halo_recv.at[k, j],
                device_id=at(o),
                device_id_type=MESH,
            )
            for j, (o, src, dst) in enumerate(moves)
        ]

    def side_columns(ks, own, halo, turn, change):
        inner = F - 2 if turn > 0 else 0
        for side in range(2):

            def one(f, carry, side=side):
                values = [colhalo[k, side, f].astype(F32) for k in ks]
                colside[side, f, pl.ds(1, H)] = change(f, *values)
                return carry

            lax.fori_loop(0, F + 2, one, 0)
            for end, place in ((0, 0), (1, H + 1)):
                for f in range(F):
                    values = [cornerhalo[k, 0, end, side, pl.ds(f, 1)] for k in ks]
                    colside[side, own + f, pl.ds(place, 1)] = change(own + f, *values)
                for f in range(2):
                    values = [cornerhalo[k, 1, end, side, pl.ds(inner + f, 1)] for k in ks]
                    colside[side, halo + f, pl.ds(place, 1)] = change(halo + f, *values)

        @pl.when(c == 0)
        def _():
            colside[0] = jnp.zeros(colside.shape[1:], F32)

        @pl.when(c == cols - 1)
        def _():
            colside[1] = jnp.zeros(colside.shape[1:], F32)

    def build(full, halo, edge, change):
        column = lax.broadcasted_iota(jnp.int32, (6, W, C), 1)

        def one(f, carry):
            for h in range(0, H + 2, 6):
                x = change(f, full[f, pl.ds(h, 6)].astype(F32))
                left = colside[0, f, pl.ds(h, 6)].reshape(6, 1, C)
                right = colside[1, f, pl.ds(h, 6)].reshape(6, 1, C)
                taps[1, f, pl.ds(h, 6)] = x.astype(BF16)
                taps[0, f, pl.ds(h, 6)] = jnp.where(
                    column == 0, left, pltpu.roll(x, 1, 1)
                ).astype(BF16)
                taps[2, f, pl.ds(h, 6)] = jnp.where(
                    column == W - 1, right, pltpu.roll(x, W - 1, 1)
                ).astype(BF16)
            return carry

        lax.fori_loop(0, F + 2, one, 0)

        @pl.when(r == 0)
        def _():
            taps[:, :, 0] = jnp.zeros((3, F + 2, W, C), BF16)

        @pl.when(r == rows - 1)
        def _():
            taps[:, :, H + 1] = jnp.zeros((3, F + 2, W, C), BF16)

        @pl.when(t == edge)
        def _():
            for f in range(2):
                for dw in range(3):
                    taps[dw, halo + f] = jnp.zeros((H + 2, W, C), BF16)

    def convolve(f, weights, back):
        left = jnp.concatenate(
            [
                taps[dw, pl.ds(f + dt, 2), pl.ds(dh, H)].reshape(2 * H * W, C)
                for dt, dh, dw in TAPS
            ],
            axis=1,
        )
        if back:
            right = jnp.concatenate([weights[26 - n] for n in range(27)], axis=1)
            return lax.dot_general(left, right, (((1,), (1,)), ((), ())), preferred_element_type=F32)
        return jnp.dot(left, weights[...].reshape(27 * C, C), preferred_element_type=F32)

    def row_of(ref, i):
        return ref[pl.ds(i, 1), :]

    def sums(x):
        return jnp.sum(x.reshape(-1, 8, C), axis=0)

    def norm_grad(values, d, mean, inverse, gain, offset):
        normed = (values - mean) * inverse
        pre = normed * gain + offset
        s = sigmoid(pre)
        e = d * s * (1.0 + pre * (1.0 - s)) * gain
        return e, sums(e), sums(e * normed)

    for load in loads[4:]:
        load.wait()
    vectors = [ref[...].reshape(1, C) for ref in (bias1, gain1, offset1, gain2, offset2)]
    bias1, gain1, offset1, gain2, offset2 = vectors

    loads[0].wait()

    def first_sums(f, carry):
        x = actf[f + 2, pl.ds(1, H)].astype(F32).reshape(H * W, C)
        put_stage(f * H * W, x)
        part[0, f] = sums(x)
        part[1, f] = sums(x * x)
        return carry

    lax.fori_loop(0, F, first_sums, 0)
    pack_rims(0)
    pl.semaphore_wait(barrier, len(everyone))
    plane_start(0)
    past = rim_copies(0, actf, 2, 0, 1)
    for copy in past:
        copy.start()
    loads[1].wait()

    def to_stage(f, carry):
        put_stage(f * H * W, cotf[f, pl.ds(1, H)].astype(F32).reshape(H * W, C))
        return carry

    lax.fori_loop(0, F, to_stage, 0)
    pack_rims(1)
    future = rim_copies(1, cotf, 0, 4, -1)
    for copy in future:
        copy.start()
    line_start(0, plane_end(0))
    stat1[...] = forward_end(0, 0)

    for copy in past:
        copy.wait_recv()

    def activate(f, x):
        shape = (1,) * (x.ndim - 1) + (C,)
        mean = row_of(stat1, f).reshape(shape)
        inverse = row_of(stat1, f + 8).reshape(shape)
        u = (x - mean) * inverse * gain1.reshape(shape) + offset1.reshape(shape)
        return u * sigmoid(u)

    side_columns((0,), 2, 0, 1, activate)
    build(actf, 0, 0, activate)
    loads[2].wait()

    def first_layer(i, carry):
        f = 2 * i
        hidden = convolve(f, w1, False)
        x = actf[pl.ds(f + 2, 2), pl.ds(1, H)].astype(F32).reshape(2 * H * W, C)
        y = (x + hidden + bias1).astype(BF16)
        layf[pl.ds(f, 2), pl.ds(1, H)] = y.reshape(2, H, W, C)
        y = y.astype(F32)
        put_stage(f * H * W, y)
        for j in range(2):
            z = y[j * H * W : (j + 1) * H * W]
            part[0, f + j] = sums(z)
            part[1, f + j] = sums(z * z)
        return carry

    lax.fori_loop(0, F // 2, first_layer, 0)
    plane_start(1)
    pack_rims(2)
    layer_rims = rim_copies(2, layf, 0, 4, -1)
    for copy in layer_rims:
        copy.start()

    for copy in future:
        copy.wait_recv()
    loads[3].wait()
    same = lambda f, x: x
    side_columns((1,), 0, 4, -1, same)
    build(cotf, 4, tms - 1, same)

    def second_grad(f):
        grad[pl.ds(f, 2)] = convolve(f, w2, True).reshape(2, H, W, C)

    second_grad(0)
    line_start(1, plane_end(1))
    second_grad(2)
    stat2[...] = forward_end(1, 1)

    def second_norm(f, carry):
        mean, inverse = row_of(stat2, f), row_of(stat2, f + 8)
        a = b = jnp.zeros((8, C), F32)
        for h in range(0, H, 8):
            v = layf[f, pl.ds(h + 1, 8)].astype(F32).reshape(8 * W, C)
            d = grad[f, pl.ds(h, 8)].reshape(8 * W, C)
            e, da, db = norm_grad(v, d, mean, inverse, gain2, offset2)
            x = cotf[f, pl.ds(h + 1, 8)].astype(F32).reshape(8 * W, C) + inverse * e
            grad[f, pl.ds(h, 8)] = x.reshape(8, W, C)
            put_stage(f * H * W + h * W, x)
            xf[f, pl.ds(h + 1, 8)] = x.astype(BF16).reshape(8, W, C)
            a, b = a + da, b + db
        part[0, f] = a
        part[1, f] = b
        return carry

    lax.fori_loop(0, F, second_norm, 0)
    plane_start(2)
    pack_rims(3)
    x_rims = rim_copies(3, xf, 0, 4, -1)
    for copy in x_rims:
        copy.start()
    line_start(2, backward_terms(2, 1))
    rest2[...] = backward_end(2)

    def settle(f, x, v):
        shape = (1,) * (x.ndim - 1) + (C,)
        r1 = row_of(rest2, f).reshape(shape)
        r2 = row_of(rest2, f + 8).reshape(shape)
        return x + (r1 + 2.0 * v * r2)

    def middle(f, carry):
        for h in range(0, H, 8):
            v = layf[f, pl.ds(h + 1, 8)].astype(F32)
            gmf[f, pl.ds(h + 1, 8)] = settle(f, grad[f, pl.ds(h, 8)], v).astype(BF16)
        return carry

    lax.fori_loop(0, F, middle, 0)
    for copy in layer_rims + x_rims:
        copy.wait_recv()

    def settle_rows(f, h, n):
        x, v = xf[f, pl.ds(h, n)].astype(F32), layf[f, pl.ds(h, n)].astype(F32)
        gmf[f, pl.ds(h, n)] = settle(f, x, v).astype(BF16)

    def middle_rows(f, carry):
        settle_rows(f, 0, 1)
        settle_rows(f, H + 1, 1)
        return carry

    def middle_frames(f, carry):
        for h in range(0, H + 2, 6):
            settle_rows(f, h, 6)
        return carry

    lax.fori_loop(0, F, middle_rows, 0)
    lax.fori_loop(F, F + 2, middle_frames, 0)
    side_columns((3, 2), 0, 4, -1, settle)

    build(gmf, 4, tms - 1, same)

    def first_grad(i, carry):
        f = 2 * i
        grad[pl.ds(f, 2)] = convolve(f, w1, True).reshape(2, H, W, C)
        return carry

    lax.fori_loop(0, F // 2, first_grad, 0)

    def first_norm(f, carry):
        mean, inverse = row_of(stat1, f + 2), row_of(stat1, f + 10)
        a = b = jnp.zeros((8, C), F32)
        for h in range(0, H, 8):
            v = actf[f + 2, pl.ds(h + 1, 8)].astype(F32).reshape(8 * W, C)
            d = grad[f, pl.ds(h, 8)].reshape(8 * W, C)
            e, da, db = norm_grad(v, d, mean, inverse, gain1, offset1)
            grad[f, pl.ds(h, 8)] = e.reshape(8, W, C)
            a, b = a + da, b + db
        part[0, f] = a
        part[1, f] = b
        return carry

    lax.fori_loop(0, F, first_norm, 0)
    plane_start(3)
    line_start(3, backward_terms(3, 0))
    rest1[...] = backward_end(3)

    def finish(f, carry):
        inverse = row_of(stat1, f + 10)
        r1, r2 = row_of(rest1, f), row_of(rest1, f + 8)
        for h in range(0, H, 8):
            v = actf[f + 2, pl.ds(h + 1, 8)].astype(F32).reshape(8 * W, C)
            e = grad[f, pl.ds(h, 8)].reshape(8 * W, C)
            x = gmf[f, pl.ds(h + 1, 8)].astype(F32).reshape(8 * W, C)
            y = x + (inverse * e + r1 + 2.0 * v * r2)
            out_ref[f, pl.ds(h, 8)] = y.astype(BF16).reshape(8, W, C)
        return carry

    lax.fori_loop(0, F, finish, 0)

    for copy in past + future + layer_rims + x_rims:
        copy.wait_send()
    for k in range(4):
        await_all(plane_in.at[k], plane_send.at[k])
        await_all(line_in.at[k], line_send.at[k])


def solution(mesh):
    sizes = tuple(mesh.shape[a] for a in AXES)
    n_plane, n_line = sizes[1] * sizes[2] - 1, sizes[0] - 1
    rims = 17
    full = (F + 2, H + 2, W, C)

    def step(act, cot, w1, b1, g1, o1, w2, g2, o2):
        hbm = pl.BlockSpec(memory_space=pltpu.HBM)
        operands = (act, cot, w1.reshape(27, C, C), w2.reshape(27, C, C), b1, g1, o1, g2, o2)
        operands = [pltpu.with_memory_space_constraint(x, pltpu.HBM) for x in operands]
        vmem = pl.BlockSpec(memory_space=pltpu.VMEM)
        return pl.pallas_call(
            functools.partial(kernel, sizes),
            name="vae_grad",
            out_shape=pltpu.VMEM((F, H, W, C), BF16),
            in_specs=[hbm] * 9,
            out_specs=vmem,
            scratch_shapes=[
                pltpu.VMEM(full, BF16),
                pltpu.VMEM(full, BF16),
                pltpu.VMEM(full, BF16),
                pltpu.VMEM((27, C, C), BF16),
                pltpu.VMEM((27, C, C), BF16),
                pltpu.VMEM((C,), F32),
                pltpu.VMEM((C,), F32),
                pltpu.VMEM((C,), F32),
                pltpu.VMEM((C,), F32),
                pltpu.VMEM((C,), F32),
                pltpu.VMEM((3,) + full, BF16),
                pltpu.VMEM((F, H, W, C), F32),
                pltpu.VMEM(full, BF16),
                pltpu.VMEM(full, BF16),
                pltpu.VMEM((2, F * H * W, 128), F32),
                pltpu.VMEM((4, 2, F, H, C), BF16),
                pltpu.VMEM((4, 2, 2, F, C), F32),
                pltpu.VMEM((4, 2, F + 2, H, C), BF16),
                pltpu.VMEM((4, 2, 2, 2, F, C), F32),
                pltpu.VMEM((2, F + 2, 24, C), F32),
                pltpu.VMEM((2, F, 8, C), F32),
                pltpu.VMEM((C, 128), BF16),
                pltpu.VMEM((128, C), BF16),
                pltpu.VMEM((16, C), F32),
                pltpu.VMEM((16, C), F32),
                pltpu.VMEM((16, C), F32),
                pltpu.VMEM((16, C), F32),
                pltpu.VMEM((2, 2, 128), F32),
                pltpu.VMEM((4, 2, 128), F32),
                pltpu.VMEM((4, 2, 128), F32),
                pltpu.VMEM((4, n_plane, 2, 128), F32),
                pltpu.VMEM((4, n_line, 2, 128), F32),
                pltpu.SemaphoreType.DMA((9,)),
                pltpu.SemaphoreType.DMA((4, rims)),
                pltpu.SemaphoreType.DMA((4, rims)),
                pltpu.SemaphoreType.DMA((4,)),
                pltpu.SemaphoreType.DMA((4,)),
                pltpu.SemaphoreType.DMA((4,)),
                pltpu.SemaphoreType.DMA((4,)),
            ],
            compiler_params=pltpu.CompilerParams(
                collective_id=0, has_side_effects=True, vmem_limit_bytes=62 << 20
            ),
        )(*operands)

    tile = P(*AXES, None)
    return jax.shard_map(
        step,
        mesh=mesh,
        in_specs=(tile, tile) + (P(),) * 7,
        out_specs=tile,
        check_vma=False,
    )
```

```python
import functools
import itertools

import jax
import jax.numpy as jnp
from jax import lax
from jax.experimental import pallas as pl
from jax.experimental.pallas import tpu as pltpu
from jax.sharding import PartitionSpec as P

MESH = pl.DeviceIdType.MESH
BF16, F32 = jnp.bfloat16, jnp.float32
EPS = 1e-6
F, H, W, C, G = 4, 16, 16, 256, 32
TAPS = tuple(itertools.product(range(3), repeat=3))
AXES = ("tm", "row", "col")
PIECES = ((1, 6), (7, 10))


def offsets_of(sizes):
    tms, rows, cols = sizes
    plane = [(0, b, d) for b in range(rows) for d in range(cols) if (b, d) != (0, 0)]
    plane.sort(key=lambda o: -(min(o[1], rows - o[1]) + min(o[2], cols - o[2])))
    line = [(a, 0, 0) for a in range(1, tms)]
    line.sort(key=lambda o: -min(o[0], tms - o[0]))
    rims = [
        (a % tms, b % rows, d % cols)
        for a in (-1, 1)
        for b in (-1, 0, 1)
        for d in (-1, 0, 1)
    ]
    everyone = list(dict.fromkeys(plane + line + rims))
    chips = [
        (a, b, d)
        for a in range(tms)
        for b in range(rows)
        for d in range(0, cols, 2)
        if (a, b, d) != (0, 0, 0)
    ]
    chips.sort(
        key=lambda o: -2 * (min(o[0], tms - o[0]) + min(o[1], rows - o[1])) - min(o[2], cols - o[2])
    )
    return plane, line, everyone, chips


def sigmoid(u):
    return 0.5 * jnp.tanh(0.5 * u) + 0.5


def split3(x):
    high = x.astype(BF16)
    rest = x - high.astype(F32)
    middle = rest.astype(BF16)
    low = (rest - middle.astype(F32)).astype(BF16)
    return jnp.concatenate([high, middle, low], axis=0)


def exact_dot(x, picks):
    n = x.shape[0]
    y = jnp.dot(split3(x), picks, preferred_element_type=F32)
    return y[:n] + y[n : 2 * n] + y[2 * n :]


def frame_of_lane(shape):
    return lax.broadcasted_iota(jnp.int32, shape, len(shape) - 1) >> 5


def over_frames(x):
    return x + pltpu.roll(x, 32, 1) + pltpu.roll(x, 64, 1) + pltpu.roll(x, 96, 1)


def running(x):
    f = frame_of_lane(x.shape)
    return (
        x
        + jnp.where(f >= 1, pltpu.roll(x, 32, 1), 0.0)
        + jnp.where(f >= 2, pltpu.roll(x, 64, 1), 0.0)
        + jnp.where(f >= 3, pltpu.roll(x, 96, 1), 0.0)
    )


def running_back(x):
    f = frame_of_lane(x.shape)
    return (
        x
        + jnp.where(f <= 2, pltpu.roll(x, 96, 1), 0.0)
        + jnp.where(f <= 1, pltpu.roll(x, 64, 1), 0.0)
        + jnp.where(f <= 0, pltpu.roll(x, 32, 1), 0.0)
    )


def kernel(
    sizes,
    act_hbm,
    cot_hbm,
    w1_hbm,
    w2_hbm,
    bias1_hbm,
    gain1_hbm,
    offset1_hbm,
    gain2_hbm,
    offset2_hbm,
    out_ref,
    actf,
    cotf,
    gmf,
    w1,
    w2,
    bias1,
    gain1,
    offset1,
    gain2,
    offset2,
    taps,
    grad,
    layf,
    xf,
    stage,
    colpack,
    cornerpack,
    colhalo,
    cornerhalo,
    colside,
    part,
    gather_m,
    spread_m,
    stat1,
    stat2,
    rest1,
    rest2,
    ends,
    mine,
    line_mine,
    plane_in,
    line_in,
    chip_mine,
    chip_brief,
    pair_in,
    near_in,
    far_in,
    in_sem,
    halo_send,
    halo_recv,
    plane_send,
    plane_recv,
    line_send,
    line_recv,
    pair_send,
    pair_recv,
    near_send,
    near_recv,
    far_send,
    far_recv,
):
    tms, rows, cols = sizes
    t, r, c = (lax.axis_index(a) for a in AXES)
    plane, line, everyone, chips = offsets_of(sizes)
    plane_cells = float(H * rows * W * cols * (C // G))

    def at(o):
        return (
            lax.rem(t + (o[0] % tms), tms),
            lax.rem(r + (o[1] % rows), rows),
            lax.rem(c + (o[2] % cols), cols),
        )

    barrier = pltpu.get_barrier_semaphore()
    for o in everyone:
        pl.semaphore_signal(barrier, inc=1, device_id=at(o), device_id_type=MESH)

    loads = [
        pltpu.make_async_copy(act_hbm, actf.at[pl.ds(2, F), pl.ds(1, H)], in_sem.at[0]),
        pltpu.make_async_copy(cot_hbm, cotf.at[pl.ds(0, F), pl.ds(1, H)], in_sem.at[1]),
        pltpu.make_async_copy(w1_hbm, w1, in_sem.at[2]),
        pltpu.make_async_copy(w2_hbm, w2, in_sem.at[3]),
        pltpu.make_async_copy(bias1_hbm, bias1, in_sem.at[4]),
        pltpu.make_async_copy(gain1_hbm, gain1, in_sem.at[5]),
        pltpu.make_async_copy(offset1_hbm, offset1, in_sem.at[6]),
        pltpu.make_async_copy(gain2_hbm, gain2, in_sem.at[7]),
        pltpu.make_async_copy(offset2_hbm, offset2, in_sem.at[8]),
    ]
    for load in loads:
        load.start()

    channel = lax.broadcasted_iota(jnp.int32, (C, 128), 0) >> 3
    group = lax.broadcasted_iota(jnp.int32, (C, 128), 1) & (G - 1)
    gather_m[...] = jnp.where(channel == group, 1.0, 0.0).astype(BF16)
    channel = lax.broadcasted_iota(jnp.int32, (128, C), 1) >> 3
    group = lax.broadcasted_iota(jnp.int32, (128, C), 0) & (G - 1)
    spread_m[...] = jnp.where(channel == group, 1.0, 0.0).astype(BF16)

    def packed_sums():
        y = exact_dot(part[...].reshape(2 * F * 8, C), gather_m[...])
        y = y.reshape(2, F, 8, 128)
        f = frame_of_lane((2, 8, 128))
        z = jnp.zeros((2, 8, 128), F32)
        for i in range(F):
            z = z + jnp.where(f == i, y[:, i], 0.0)
        return jnp.sum(z, axis=1)

    def plane_copy(k, j):
        return pltpu.make_async_remote_copy(
            src_ref=mine.at[k],
            dst_ref=plane_in.at[k, j],
            send_sem=plane_send.at[k],
            recv_sem=plane_recv.at[k],
            device_id=at(plane[j]),
            device_id_type=MESH,
        )

    def line_copy(k, j):
        return pltpu.make_async_remote_copy(
            src_ref=line_mine.at[k],
            dst_ref=line_in.at[k, line[j][0] - 1],
            send_sem=line_send.at[k],
            recv_sem=line_recv.at[k],
            device_id=at(line[j]),
            device_id_type=MESH,
        )

    def await_all(buffer, sem):
        pltpu.make_async_copy(buffer, buffer, sem).wait()

    def plane_start(k):
        for j in range(len(plane)):
            plane_copy(k, j).start()

    def plane_end(k):
        await_all(plane_in.at[k], plane_recv.at[k])
        return mine[k] + jnp.sum(plane_in[k], axis=0)

    def line_start(k, value):
        line_mine[k] = value
        for j in range(len(line)):
            line_copy(k, j).start()

    def line_end(k):
        await_all(line_in.at[k], line_recv.at[k])
        return [line_in[k, j] for j in range(len(line))]

    def counts(first_frame):
        f = first_frame + frame_of_lane((1, 128)) + 1
        return jnp.maximum(f, 1).astype(F32) * plane_cells

    def moments(prefix, n):
        mean = prefix[0:1] / n
        return mean, lax.rsqrt(prefix[1:2] / n - mean * mean + EPS)

    def spread(first, second, before=None, after=None):
        row = lax.broadcasted_iota(jnp.int32, (8, 128), 0)
        f = frame_of_lane((8, 128))
        halves = []
        for i, own in enumerate((first, second)):
            own = jnp.broadcast_to(own, (8, 128))
            if before is not None:
                ahead = jnp.broadcast_to(before[i], (8, 128))
                frame = jnp.where(row < 2, row + 2, row - 2)
                own = jnp.where(row < 2, ahead, own)
            elif after is not None:
                behind = jnp.broadcast_to(after[i], (8, 128))
                frame = jnp.where(row < F, row, row - F)
                own = jnp.where(row < F, own, behind)
            else:
                frame = row
            halves.append(jnp.where(f == frame, own, 0.0))
        return exact_dot(jnp.concatenate(halves, axis=0), spread_m[...])

    def first_end():
        got = line_end(0)
        zero = jnp.zeros((2, 128), F32)
        near = jnp.where(t >= 1, got[0], zero)
        far = zero
        for j in range(1, len(line)):
            far = far + jnp.where(t >= j + 1, got[j], zero)
        own = moments(over_frames(far + near) + running(line_mine[0]), counts(t * F))
        ends[0, 0:1] = own[0]
        ends[0, 1:2] = own[1]
        before = moments(over_frames(far) + running(near), counts(t * F - F))
        return spread(own[0], own[1], before)

    def partner_copy(k):
        return pltpu.make_async_remote_copy(
            src_ref=mine.at[k],
            dst_ref=pair_in.at[k],
            send_sem=pair_send.at[k],
            recv_sem=pair_recv.at[k],
            device_id=(t, r, c + 1 - 2 * lax.rem(c, 2)),
            device_id_type=MESH,
        )

    def chip_copy(k, o):
        inside = o[0] == 0
        place = o[1] * (cols // 2) + o[2] // 2
        return pltpu.make_async_remote_copy(
            src_ref=chip_mine.at[k] if inside else chip_brief.at[k],
            dst_ref=near_in.at[k, place - 1] if inside else far_in.at[k, o[0] - 1, place],
            send_sem=(near_send if inside else far_send).at[k],
            recv_sem=(near_recv if inside else far_recv).at[k],
            device_id=at(o),
            device_id_type=MESH,
        )

    def chip_start(k, value):
        mine[k] = value
        pair = partner_copy(k)
        pair.start()
        pair.wait_recv()
        value = value + pair_in[k]
        chip_mine[k] = value
        f = frame_of_lane((1, 128))
        whole = over_frames(value)
        first = jnp.where(f == 2, pltpu.roll(value, 64, 1)[0:1], pltpu.roll(value, 96, 1)[1:2])
        both = jnp.where(f == 0, whole[0:1], whole[1:2])
        chip_brief[k] = jnp.where(f < 2, both, first)
        for o in chips:
            chip_copy(k, o).start()
        pair.wait_send()

    def chip_end(k):
        await_all(near_in.at[k], near_recv.at[k])
        own = chip_mine[k] + jnp.sum(near_in[k], axis=0)
        await_all(far_in.at[k], far_recv.at[k])
        return own, [jnp.sum(far_in[k, a], axis=0) for a in range(tms - 1)]

    def widen(x):
        f = frame_of_lane((1, 128))
        rows = [jnp.where(f == i, x, 0.0) for i in range(2)]
        return over_frames(jnp.concatenate(rows, axis=0))

    def forward_end(k, layer):
        own, got = chip_end(k)
        earlier = jnp.zeros((1, 128), F32)
        for j in range(tms - 1):
            earlier = earlier + jnp.where(t >= j + 1, got[j], 0.0)
        own = moments(widen(earlier) + running(own), counts(t * F))
        ends[layer, 0:1] = own[0]
        ends[layer, 1:2] = own[1]
        return spread(own[0], own[1])

    def backward_terms(totals, layer):
        mean, inverse = ends[layer, 0:1], ends[layer, 1:2]
        n = counts(t * F)
        a, b = totals[0:1], totals[1:2]
        first = (-inverse * a + b * inverse * inverse * mean) / n
        second = -0.5 * b * inverse * inverse / n
        return jnp.concatenate([first, second], axis=0)

    def backward_end(k):
        own, got = chip_end(k)
        near = jnp.where(t < tms - 1, got[-1], 0.0)
        later = near
        for j in range(tms - 2):
            later = later + jnp.where(t < j + 1, got[j], 0.0)
        later = widen(later)
        f = frame_of_lane((1, 128))
        first = jnp.concatenate([pltpu.roll(near, 96, 1), pltpu.roll(near, 64, 1)], axis=0)
        behind = later - jnp.where(f == 1, first, 0.0)
        rest = later + running_back(own)
        return spread(rest[0:1], rest[1:2], after=(behind[0:1], behind[1:2]))

    def put_stage(start, x):
        for i in range(2):
            stage[i, pl.ds(start, x.shape[0])] = x[:, i * 128 : i * 128 + 128]

    def fill_stage(full):
        def one(f, carry):
            put_stage(f * H * W, full[f, pl.ds(1, H)].astype(F32).reshape(H * W, C))
            return carry

        lax.fori_loop(0, F, one, 0)

    def staged(start, size, stride):
        return jnp.concatenate(
            [stage[i, pl.ds(start, size, stride=stride), :] for i in range(2)], axis=1
        )

    def pack_rims(k):
        for side, column in enumerate((0, W - 1)):
            for f in range(F):
                rim = staged(f * H * W + column, H, W)
                colpack[k, side, f] = rim.astype(BF16)
            for end, line_at in enumerate((0, H - 1)):
                cornerpack[k, end, side] = staged(line_at * W + column, F, H * W)

    def rim_copies(k, full, own, halo, turn):
        last = own + (F - 2 if turn > 0 else 0)
        inner = F - 2 if turn > 0 else 0
        moves = []
        for start, n in PIECES:
            src = full.at[pl.ds(last, 2), pl.ds(start, n)]
            moves.append(((turn, 0, 0), src, full.at[pl.ds(halo, 2), pl.ds(start, n)]))
        for step, src, dst in ((1, H, 0), (-1, 1, H + 1)):
            moves.append(((0, step, 0), full.at[pl.ds(own, F), src], full.at[pl.ds(own, F), dst]))
            moves.append(((turn, step, 0), full.at[pl.ds(last, 2), src], full.at[pl.ds(halo, 2), dst]))
        for step, src, dst in ((1, 1, 0), (-1, 0, 1)):
            moves.append(((0, 0, step), colpack.at[k, src], colhalo.at[k, dst, pl.ds(own, F)]))
            moves.append(
                ((turn, 0, step), colpack.at[k, src, pl.ds(inner, 2)], colhalo.at[k, dst, pl.ds(halo, 2)])
            )
        for down, over in itertools.product((1, -1), repeat=2):
            src = cornerpack.at[k, int(down > 0), int(over > 0)]
            place = (int(down < 0), int(over < 0))
            moves.append(((0, down, over), src, cornerhalo.at[k, 0, place[0], place[1]]))
            moves.append(((turn, down, over), src, cornerhalo.at[k, 1, place[0], place[1]]))
        return [
            pltpu.make_async_remote_copy(
                src_ref=src,
                dst_ref=dst,
                send_sem=halo_send.at[k, j],
                recv_sem=halo_recv.at[k, j],
                device_id=at(o),
                device_id_type=MESH,
            )
            for j, (o, src, dst) in enumerate(moves)
        ]

    def side_columns(ks, own, halo, turn, change):
        inner = F - 2 if turn > 0 else 0
        for side in range(2):

            def one(f, carry, side=side):
                values = [colhalo[k, side, f].astype(F32) for k in ks]
                colside[side, f, pl.ds(1, H)] = change(f, *values)
                return carry

            lax.fori_loop(0, F + 2, one, 0)
            for end, place in ((0, 0), (1, H + 1)):
                for f in range(F):
                    values = [cornerhalo[k, 0, end, side, pl.ds(f, 1)] for k in ks]
                    colside[side, own + f, pl.ds(place, 1)] = change(own + f, *values)
                for f in range(2):
                    values = [cornerhalo[k, 1, end, side, pl.ds(inner + f, 1)] for k in ks]
                    colside[side, halo + f, pl.ds(place, 1)] = change(halo + f, *values)

        @pl.when(c == 0)
        def _():
            colside[0] = jnp.zeros(colside.shape[1:], F32)

        @pl.when(c == cols - 1)
        def _():
            colside[1] = jnp.zeros(colside.shape[1:], F32)

    def build(full, halo, edge, change):
        column = lax.broadcasted_iota(jnp.int32, (6, W, C), 1)

        def one(f, carry):
            for h in range(0, H + 2, 6):
                x = change(f, full[f, pl.ds(h, 6)].astype(F32))
                left = colside[0, f, pl.ds(h, 6)].reshape(6, 1, C)
                right = colside[1, f, pl.ds(h, 6)].reshape(6, 1, C)
                taps[1, f, pl.ds(h, 6)] = x.astype(BF16)
                taps[0, f, pl.ds(h, 6)] = jnp.where(
                    column == 0, left, pltpu.roll(x, 1, 1)
                ).astype(BF16)
                taps[2, f, pl.ds(h, 6)] = jnp.where(
                    column == W - 1, right, pltpu.roll(x, W - 1, 1)
                ).astype(BF16)
            return carry

        lax.fori_loop(0, F + 2, one, 0)

        @pl.when(r == 0)
        def _():
            taps[:, :, 0] = jnp.zeros((3, F + 2, W, C), BF16)

        @pl.when(r == rows - 1)
        def _():
            taps[:, :, H + 1] = jnp.zeros((3, F + 2, W, C), BF16)

        @pl.when(t == edge)
        def _():
            for f in range(2):
                for dw in range(3):
                    taps[dw, halo + f] = jnp.zeros((H + 2, W, C), BF16)

    def convolve(f, weights, back):
        left = jnp.concatenate(
            [
                taps[dw, pl.ds(f + dt, 2), pl.ds(dh, H)].reshape(2 * H * W, C)
                for dt, dh, dw in TAPS
            ],
            axis=1,
        )
        if back:
            right = jnp.concatenate([weights[26 - n] for n in range(27)], axis=1)
            return lax.dot_general(left, right, (((1,), (1,)), ((), ())), preferred_element_type=F32)
        return jnp.dot(left, weights[...].reshape(27 * C, C), preferred_element_type=F32)

    def row_of(ref, i):
        return ref[pl.ds(i, 1), :]

    def sums(x):
        return jnp.sum(x.reshape(-1, 8, C), axis=0)

    def norm_grad(values, d, mean, inverse, gain, offset):
        normed = (values - mean) * inverse
        pre = normed * gain + offset
        s = sigmoid(pre)
        e = d * s * (1.0 + pre * (1.0 - s)) * gain
        return e, sums(e), sums(e * normed)

    for load in loads[4:]:
        load.wait()
    vectors = [ref[...].reshape(1, C) for ref in (bias1, gain1, offset1, gain2, offset2)]
    bias1, gain1, offset1, gain2, offset2 = vectors

    loads[0].wait()

    def first_sums(f, carry):
        x = actf[f + 2, pl.ds(1, H)].astype(F32).reshape(H * W, C)
        put_stage(f * H * W, x)
        part[0, f] = sums(x)
        part[1, f] = sums(x * x)
        return carry

    lax.fori_loop(0, F, first_sums, 0)
    mine[0] = packed_sums()
    pl.semaphore_wait(barrier, len(everyone))
    plane_start(0)
    past = rim_copies(0, actf, 2, 0, 1)
    for copy in past[1:6]:
        copy.start()
    pack_rims(0)
    for copy in past[6:]:
        copy.start()
    loads[1].wait()
    fill_stage(cotf)
    pack_rims(1)
    line_start(0, plane_end(0))
    past[0].start()
    future = rim_copies(1, cotf, 0, 4, -1)
    for copy in future:
        copy.start()
    stat1[...] = first_end()

    for copy in past:
        copy.wait_recv()

    def activate(f, x):
        shape = (1,) * (x.ndim - 1) + (C,)
        mean = row_of(stat1, f).reshape(shape)
        inverse = row_of(stat1, f + 8).reshape(shape)
        u = (x - mean) * inverse * gain1.reshape(shape) + offset1.reshape(shape)
        return u * sigmoid(u)

    side_columns((0,), 2, 0, 1, activate)
    build(actf, 0, 0, activate)
    loads[2].wait()

    def first_layer(i, carry):
        f = 2 * i
        hidden = convolve(f, w1, False)
        x = actf[pl.ds(f + 2, 2), pl.ds(1, H)].astype(F32).reshape(2 * H * W, C)
        y = (x + hidden + bias1).astype(BF16)
        layf[pl.ds(f, 2), pl.ds(1, H)] = y.reshape(2, H, W, C)
        y = y.astype(F32)
        for j in range(2):
            z = y[j * H * W : (j + 1) * H * W]
            part[0, f + j] = sums(z)
            part[1, f + j] = sums(z * z)
        return carry

    lax.fori_loop(0, F // 2, first_layer, 0)
    chip_start(1, packed_sums())
    layer_rims = rim_copies(2, layf, 0, 4, -1)
    for copy in layer_rims[:6]:
        copy.start()
    fill_stage(layf)
    pack_rims(2)
    for copy in layer_rims[6:]:
        copy.start()

    for copy in future:
        copy.wait_recv()
    loads[3].wait()
    same = lambda f, x: x
    side_columns((1,), 0, 4, -1, same)
    build(cotf, 4, tms - 1, same)

    def second_grad(f):
        grad[pl.ds(f, 2)] = convolve(f, w2, True).reshape(2, H, W, C)

    second_grad(0)
    second_grad(2)
    stat2[...] = forward_end(1, 1)

    def second_norm(f, carry):
        mean, inverse = row_of(stat2, f), row_of(stat2, f + 8)
        a = b = jnp.zeros((8, C), F32)
        for h in range(0, H, 8):
            v = layf[f, pl.ds(h + 1, 8)].astype(F32).reshape(8 * W, C)
            d = grad[f, pl.ds(h, 8)].reshape(8 * W, C)
            e, da, db = norm_grad(v, d, mean, inverse, gain2, offset2)
            x = cotf[f, pl.ds(h + 1, 8)].astype(F32).reshape(8 * W, C) + inverse * e
            grad[f, pl.ds(h, 8)] = x.reshape(8, W, C)
            xf[f, pl.ds(h + 1, 8)] = x.astype(BF16).reshape(8, W, C)
            a, b = a + da, b + db
        part[0, f] = a
        part[1, f] = b
        return carry

    lax.fori_loop(0, F, second_norm, 0)
    chip_start(2, backward_terms(packed_sums(), 1))
    x_rims = rim_copies(3, xf, 0, 4, -1)
    for copy in x_rims[:6]:
        copy.start()
    fill_stage(xf)
    pack_rims(3)
    for copy in x_rims[6:]:
        copy.start()
    rest2[...] = backward_end(2)

    def settle(f, x, v):
        shape = (1,) * (x.ndim - 1) + (C,)
        r1 = row_of(rest2, f).reshape(shape)
        r2 = row_of(rest2, f + 8).reshape(shape)
        return x + (r1 + 2.0 * v * r2)

    def middle(f, carry):
        for h in range(0, H, 8):
            v = layf[f, pl.ds(h + 1, 8)].astype(F32)
            gmf[f, pl.ds(h + 1, 8)] = settle(f, grad[f, pl.ds(h, 8)], v).astype(BF16)
        return carry

    lax.fori_loop(0, F, middle, 0)
    for copy in layer_rims + x_rims:
        copy.wait_recv()

    def settle_rows(f, h, n):
        x, v = xf[f, pl.ds(h, n)].astype(F32), layf[f, pl.ds(h, n)].astype(F32)
        gmf[f, pl.ds(h, n)] = settle(f, x, v).astype(BF16)

    def middle_rows(f, carry):
        settle_rows(f, 0, 1)
        settle_rows(f, H + 1, 1)
        return carry

    def middle_frames(f, carry):
        for h in range(0, H + 2, 6):
            settle_rows(f, h, 6)
        return carry

    lax.fori_loop(0, F, middle_rows, 0)
    lax.fori_loop(F, F + 2, middle_frames, 0)
    side_columns((3, 2), 0, 4, -1, settle)

    build(gmf, 4, tms - 1, same)

    def first_grad(i, carry):
        f = 2 * i
        grad[pl.ds(f, 2)] = convolve(f, w1, True).reshape(2, H, W, C)
        return carry

    lax.fori_loop(0, F // 2, first_grad, 0)

    def first_norm(f, carry):
        mean, inverse = row_of(stat1, f + 2), row_of(stat1, f + 10)
        a = b = jnp.zeros((8, C), F32)
        for h in range(0, H, 8):
            v = actf[f + 2, pl.ds(h + 1, 8)].astype(F32).reshape(8 * W, C)
            d = grad[f, pl.ds(h, 8)].reshape(8 * W, C)
            e, da, db = norm_grad(v, d, mean, inverse, gain1, offset1)
            grad[f, pl.ds(h, 8)] = e.reshape(8, W, C)
            a, b = a + da, b + db
        part[0, f] = a
        part[1, f] = b
        return carry

    lax.fori_loop(0, F, first_norm, 0)
    chip_start(3, backward_terms(packed_sums(), 0))
    rest1[...] = backward_end(3)

    def finish(f, carry):
        inverse = row_of(stat1, f + 10)
        r1, r2 = row_of(rest1, f), row_of(rest1, f + 8)
        for h in range(0, H, 8):
            v = actf[f + 2, pl.ds(h + 1, 8)].astype(F32).reshape(8 * W, C)
            e = grad[f, pl.ds(h, 8)].reshape(8 * W, C)
            x = gmf[f, pl.ds(h + 1, 8)].astype(F32).reshape(8 * W, C)
            y = x + (inverse * e + r1 + 2.0 * v * r2)
            out_ref[f, pl.ds(h, 8)] = y.astype(BF16).reshape(8, W, C)
        return carry

    lax.fori_loop(0, F, finish, 0)

    for copy in past + future + layer_rims + x_rims:
        copy.wait_send()
    await_all(plane_in.at[0], plane_send.at[0])
    await_all(line_in.at[0], line_send.at[0])
    for k in range(1, 4):
        await_all(near_in.at[k], near_send.at[k])
        await_all(far_in.at[k], far_send.at[k])


def solution(mesh):
    sizes = tuple(mesh.shape[a] for a in AXES)
    n_plane, n_line = sizes[1] * sizes[2] - 1, sizes[0] - 1
    n_chips = sizes[1] * sizes[2] // 2
    rims = 18
    full = (F + 2, H + 2, W, C)

    def step(act, cot, w1, b1, g1, o1, w2, g2, o2):
        hbm = pl.BlockSpec(memory_space=pltpu.HBM)
        operands = (act, cot, w1.reshape(27, C, C), w2.reshape(27, C, C), b1, g1, o1, g2, o2)
        operands = [pltpu.with_memory_space_constraint(x, pltpu.HBM) for x in operands]
        vmem = pl.BlockSpec(memory_space=pltpu.VMEM)
        return pl.pallas_call(
            functools.partial(kernel, sizes),
            name="vae_grad",
            out_shape=pltpu.VMEM((F, H, W, C), BF16),
            in_specs=[hbm] * 9,
            out_specs=vmem,
            scratch_shapes=[
                pltpu.VMEM(full, BF16),
                pltpu.VMEM(full, BF16),
                pltpu.VMEM(full, BF16),
                pltpu.VMEM((27, C, C), BF16),
                pltpu.VMEM((27, C, C), BF16),
                pltpu.VMEM((C,), F32),
                pltpu.VMEM((C,), F32),
                pltpu.VMEM((C,), F32),
                pltpu.VMEM((C,), F32),
                pltpu.VMEM((C,), F32),
                pltpu.VMEM((3,) + full, BF16),
                pltpu.VMEM((F, H, W, C), F32),
                pltpu.VMEM(full, BF16),
                pltpu.VMEM(full, BF16),
                pltpu.VMEM((2, F * H * W, 128), F32),
                pltpu.VMEM((4, 2, F, H, C), BF16),
                pltpu.VMEM((4, 2, 2, F, C), F32),
                pltpu.VMEM((4, 2, F + 2, H, C), BF16),
                pltpu.VMEM((4, 2, 2, 2, F, C), F32),
                pltpu.VMEM((2, F + 2, 24, C), F32),
                pltpu.VMEM((2, F, 8, C), F32),
                pltpu.VMEM((C, 128), BF16),
                pltpu.VMEM((128, C), BF16),
                pltpu.VMEM((16, C), F32),
                pltpu.VMEM((16, C), F32),
                pltpu.VMEM((16, C), F32),
                pltpu.VMEM((16, C), F32),
                pltpu.VMEM((2, 2, 128), F32),
                pltpu.VMEM((4, 2, 128), F32),
                pltpu.VMEM((4, 2, 128), F32),
                pltpu.VMEM((1, n_plane, 2, 128), F32),
                pltpu.VMEM((1, n_line, 2, 128), F32),
                pltpu.VMEM((4, 2, 128), F32),
                pltpu.VMEM((4, 1, 128), F32),
                pltpu.VMEM((4, 2, 128), F32),
                pltpu.VMEM((4, n_chips - 1, 2, 128), F32),
                pltpu.VMEM((4, n_line, n_chips, 1, 128), F32),
                pltpu.SemaphoreType.DMA((9,)),
                pltpu.SemaphoreType.DMA((4, rims)),
                pltpu.SemaphoreType.DMA((4, rims)),
                *[pltpu.SemaphoreType.DMA((4,))] * 10,
            ],
            compiler_params=pltpu.CompilerParams(
                collective_id=0, has_side_effects=True, vmem_limit_bytes=62 << 20
            ),
        )(*operands)

    tile = P(*AXES, None)
    return jax.shard_map(
        step,
        mesh=mesh,
        in_specs=(tile, tile) + (P(),) * 7,
        out_specs=tile,
        check_vma=False,
    )
```

```python
import functools
import itertools

import jax
import jax.numpy as jnp
from jax import lax
from jax.experimental import pallas as pl
from jax.experimental.pallas import tpu as pltpu
from jax.sharding import PartitionSpec as P

MESH = pl.DeviceIdType.MESH
BF16, F32 = jnp.bfloat16, jnp.float32
EPS = 1e-6
F, H, W, C, G = 4, 16, 16, 256, 32
TAPS = tuple(itertools.product(range(3), repeat=3))
AXES = ("tm", "row", "col")
PIECES = ((1, 6), (7, 10))


def offsets_of(sizes):
    tms, rows, cols = sizes
    plane = [(0, b, d) for b in range(rows) for d in range(cols) if (b, d) != (0, 0)]
    plane.sort(key=lambda o: -(min(o[1], rows - o[1]) + min(o[2], cols - o[2])))
    line = [(a, 0, 0) for a in range(1, tms)]
    line.sort(key=lambda o: -min(o[0], tms - o[0]))
    rims = [
        (a % tms, b % rows, d % cols)
        for a in (-1, 1)
        for b in (-1, 0, 1)
        for d in (-1, 0, 1)
    ]
    everyone = list(dict.fromkeys(plane + line + rims))
    chips = [
        (a, b, d)
        for a in range(tms)
        for b in range(rows)
        for d in range(0, cols, 2)
        if (a, b, d) != (0, 0, 0)
    ]
    chips.sort(
        key=lambda o: -2 * (min(o[0], tms - o[0]) + min(o[1], rows - o[1])) - min(o[2], cols - o[2])
    )
    return plane, line, everyone, chips


def sigmoid(u):
    return 0.5 * jnp.tanh(0.5 * u) + 0.5


def split3(x):
    high = x.astype(BF16)
    rest = x - high.astype(F32)
    middle = rest.astype(BF16)
    low = (rest - middle.astype(F32)).astype(BF16)
    return jnp.concatenate([high, middle, low], axis=0)


def exact_dot(x, picks):
    n = x.shape[0]
    y = jnp.dot(split3(x), picks, preferred_element_type=F32)
    return y[:n] + y[n : 2 * n] + y[2 * n :]


def frame_of_lane(shape):
    return lax.broadcasted_iota(jnp.int32, shape, len(shape) - 1) >> 5


def over_frames(x):
    return x + pltpu.roll(x, 32, 1) + pltpu.roll(x, 64, 1) + pltpu.roll(x, 96, 1)


def running(x):
    f = frame_of_lane(x.shape)
    return (
        x
        + jnp.where(f >= 1, pltpu.roll(x, 32, 1), 0.0)
        + jnp.where(f >= 2, pltpu.roll(x, 64, 1), 0.0)
        + jnp.where(f >= 3, pltpu.roll(x, 96, 1), 0.0)
    )


def running_back(x):
    f = frame_of_lane(x.shape)
    return (
        x
        + jnp.where(f <= 2, pltpu.roll(x, 96, 1), 0.0)
        + jnp.where(f <= 1, pltpu.roll(x, 64, 1), 0.0)
        + jnp.where(f <= 0, pltpu.roll(x, 32, 1), 0.0)
    )


def kernel(
    sizes,
    act_hbm,
    cot_hbm,
    w1_hbm,
    w2_hbm,
    bias1_hbm,
    gain1_hbm,
    offset1_hbm,
    gain2_hbm,
    offset2_hbm,
    out_ref,
    actf,
    cotf,
    gmf,
    w1,
    w2,
    bias1,
    gain1,
    offset1,
    gain2,
    offset2,
    taps,
    grad,
    layf,
    xf,
    stage,
    colpack,
    cornerpack,
    colhalo,
    cornerhalo,
    colside,
    part,
    gather_m,
    spread_m,
    stat1,
    stat2,
    rest1,
    rest2,
    ends,
    mine,
    line_mine,
    plane_in,
    line_in,
    chip_mine,
    chip_brief,
    pair_in,
    near_in,
    far_in,
    arrived,
    in_sem,
    halo_send,
    halo_recv,
    plane_send,
    plane_recv,
    line_send,
    line_recv,
    pair_send,
    pair_recv,
    near_send,
    near_recv,
    far_send,
    far_recv,
):
    tms, rows, cols = sizes
    t, r, c = (lax.axis_index(a) for a in AXES)
    plane, line, everyone, chips = offsets_of(sizes)
    plane_cells = float(H * rows * W * cols * (C // G))

    def at(o):
        return (
            lax.rem(t + (o[0] % tms), tms),
            lax.rem(r + (o[1] % rows), rows),
            lax.rem(c + (o[2] % cols), cols),
        )

    barrier = pltpu.get_barrier_semaphore()
    for o in everyone:
        pl.semaphore_signal(barrier, inc=1, device_id=at(o), device_id_type=MESH)

    loads = [
        pltpu.make_async_copy(act_hbm, actf.at[pl.ds(2, F), pl.ds(1, H)], in_sem.at[0]),
        pltpu.make_async_copy(cot_hbm, cotf.at[pl.ds(0, F), pl.ds(1, H)], in_sem.at[1]),
        pltpu.make_async_copy(w1_hbm, w1, in_sem.at[2]),
        pltpu.make_async_copy(w2_hbm, w2, in_sem.at[3]),
        pltpu.make_async_copy(bias1_hbm, bias1, in_sem.at[4]),
        pltpu.make_async_copy(gain1_hbm, gain1, in_sem.at[5]),
        pltpu.make_async_copy(offset1_hbm, offset1, in_sem.at[6]),
        pltpu.make_async_copy(gain2_hbm, gain2, in_sem.at[7]),
        pltpu.make_async_copy(offset2_hbm, offset2, in_sem.at[8]),
    ]
    for load in loads:
        load.start()

    channel = lax.broadcasted_iota(jnp.int32, (C, 128), 0) >> 3
    group = lax.broadcasted_iota(jnp.int32, (C, 128), 1) & (G - 1)
    gather_m[...] = jnp.where(channel == group, 1.0, 0.0).astype(BF16)
    channel = lax.broadcasted_iota(jnp.int32, (128, C), 1) >> 3
    group = lax.broadcasted_iota(jnp.int32, (128, C), 0) & (G - 1)
    spread_m[...] = jnp.where(channel == group, 1.0, 0.0).astype(BF16)

    def packed_sums():
        y = exact_dot(part[...].reshape(2 * F * 8, C), gather_m[...])
        y = y.reshape(2, F, 8, 128)
        f = frame_of_lane((2, 8, 128))
        z = jnp.zeros((2, 8, 128), F32)
        for i in range(F):
            z = z + jnp.where(f == i, y[:, i], 0.0)
        return jnp.sum(z, axis=1)

    def plane_copy(k, j):
        return pltpu.make_async_remote_copy(
            src_ref=mine.at[k],
            dst_ref=plane_in.at[k, j],
            send_sem=plane_send.at[k],
            recv_sem=plane_recv.at[k],
            device_id=at(plane[j]),
            device_id_type=MESH,
        )

    def line_copy(k, j):
        return pltpu.make_async_remote_copy(
            src_ref=line_mine.at[k],
            dst_ref=line_in.at[k, line[j][0] - 1],
            send_sem=line_send.at[k],
            recv_sem=line_recv.at[k],
            device_id=at(line[j]),
            device_id_type=MESH,
        )

    def await_all(buffer, sem):
        pltpu.make_async_copy(buffer, buffer, sem).wait()

    def plane_start(k):
        for j in range(len(plane)):
            plane_copy(k, j).start()

    def plane_end(k):
        await_all(plane_in.at[k], plane_recv.at[k])
        return mine[k] + jnp.sum(plane_in[k], axis=0)

    def line_start(k, value):
        line_mine[k] = value
        for j in range(len(line)):
            line_copy(k, j).start()

    def line_end(k):
        await_all(line_in.at[k], line_recv.at[k])
        return [line_in[k, j] for j in range(len(line))]

    def counts(first_frame):
        f = first_frame + frame_of_lane((1, 128)) + 1
        return jnp.maximum(f, 1).astype(F32) * plane_cells

    def moments(prefix, n):
        mean = prefix[0:1] / n
        return mean, lax.rsqrt(prefix[1:2] / n - mean * mean + EPS)

    def spread(first, second, before=None, after=None):
        row = lax.broadcasted_iota(jnp.int32, (8, 128), 0)
        f = frame_of_lane((8, 128))
        halves = []
        for i, own in enumerate((first, second)):
            own = jnp.broadcast_to(own, (8, 128))
            if before is not None:
                ahead = jnp.broadcast_to(before[i], (8, 128))
                frame = jnp.where(row < 2, row + 2, row - 2)
                own = jnp.where(row < 2, ahead, own)
            elif after is not None:
                behind = jnp.broadcast_to(after[i], (8, 128))
                frame = jnp.where(row < F, row, row - F)
                own = jnp.where(row < F, own, behind)
            else:
                frame = row
            halves.append(jnp.where(f == frame, own, 0.0))
        return exact_dot(jnp.concatenate(halves, axis=0), spread_m[...])

    def first_end():
        got = line_end(0)
        zero = jnp.zeros((2, 128), F32)
        near = jnp.where(t >= 1, got[0], zero)
        far = zero
        for j in range(1, len(line)):
            far = far + jnp.where(t >= j + 1, got[j], zero)
        own = moments(over_frames(far + near) + running(line_mine[0]), counts(t * F))
        ends[0, 0:1] = own[0]
        ends[0, 1:2] = own[1]
        before = moments(over_frames(far) + running(near), counts(t * F - F))
        return spread(own[0], own[1], before)

    def partner_copy(k):
        return pltpu.make_async_remote_copy(
            src_ref=mine.at[k],
            dst_ref=pair_in.at[k],
            send_sem=pair_send.at[k],
            recv_sem=pair_recv.at[k],
            device_id=(t, r, c + 1 - 2 * lax.rem(c, 2)),
            device_id_type=MESH,
        )

    def chip_copy(k, o):
        inside = o[0] == 0
        place = o[1] * (cols // 2) + o[2] // 2
        return pltpu.make_async_remote_copy(
            src_ref=chip_mine.at[k] if inside else chip_brief.at[k],
            dst_ref=near_in.at[k, place - 1] if inside else far_in.at[k, o[0] - 1, place],
            send_sem=near_send.at[k] if inside else far_send.at[k, o[0] - 1],
            recv_sem=near_recv.at[k] if inside else far_recv.at[k, o[0] - 1],
            device_id=at(o),
            device_id_type=MESH,
        )

    def goes(a, forward):
        return t + a < tms if forward else t + a >= tms

    def comes(a, forward):
        return t >= a if forward else t < a

    steps = sorted(range(1, tms), key=lambda a: -min(a, tms - a))

    def chip_start(k, value, forward):
        mine[k] = value
        pair = partner_copy(k)
        pair.start()
        pair.wait_recv()
        value = value + pair_in[k]
        chip_mine[k] = value
        f = frame_of_lane((1, 128))
        whole = over_frames(value)
        first = jnp.where(f == 2, pltpu.roll(value, 64, 1)[0:1], pltpu.roll(value, 96, 1)[1:2])
        both = jnp.where(f == 0, whole[0:1], whole[1:2])
        chip_brief[k] = jnp.where(f < 2, both, first)
        for a in steps:

            @pl.when(goes(a, forward))
            def _(a=a):
                for o in chips:
                    if o[0] == a:
                        chip_copy(k, o).start()

        for o in chips:
            if o[0] == 0:
                chip_copy(k, o).start()
        pair.wait_send()

    def chip_end(k, forward):
        arrived[...] = jnp.zeros(arrived.shape, F32)
        await_all(near_in.at[k], near_recv.at[k])
        own = chip_mine[k] + jnp.sum(near_in[k], axis=0)
        for a in reversed(steps):

            @pl.when(comes(a, forward))
            def _(a=a):
                await_all(far_in.at[k, a - 1], far_recv.at[k, a - 1])
                arrived[a - 1] = jnp.sum(far_in[k, a - 1], axis=0)

        return own, [arrived[a] for a in range(tms - 1)]

    def widen(x):
        f = frame_of_lane((1, 128))
        rows = [jnp.where(f == i, x, 0.0) for i in range(2)]
        return over_frames(jnp.concatenate(rows, axis=0))

    def forward_end(k, layer):
        own, got = chip_end(k, True)
        earlier = sum(got[1:], got[0])
        own = moments(widen(earlier) + running(own), counts(t * F))
        ends[layer, 0:1] = own[0]
        ends[layer, 1:2] = own[1]
        return spread(own[0], own[1])

    def backward_terms(totals, layer):
        mean, inverse = ends[layer, 0:1], ends[layer, 1:2]
        n = counts(t * F)
        a, b = totals[0:1], totals[1:2]
        first = (-inverse * a + b * inverse * inverse * mean) / n
        second = -0.5 * b * inverse * inverse / n
        return jnp.concatenate([first, second], axis=0)

    def backward_end(k):
        own, got = chip_end(k, False)
        near = got[-1]
        later = widen(sum(got[1:], got[0]))
        f = frame_of_lane((1, 128))
        first = jnp.concatenate([pltpu.roll(near, 96, 1), pltpu.roll(near, 64, 1)], axis=0)
        behind = later - jnp.where(f == 1, first, 0.0)
        rest = later + running_back(own)
        return spread(rest[0:1], rest[1:2], after=(behind[0:1], behind[1:2]))

    def put_stage(start, x):
        for i in range(2):
            stage[i, pl.ds(start, x.shape[0])] = x[:, i * 128 : i * 128 + 128]

    def fill_stage(full):
        def one(f, carry):
            put_stage(f * H * W, full[f, pl.ds(1, H)].astype(F32).reshape(H * W, C))
            return carry

        lax.fori_loop(0, F, one, 0)

    def staged(start, size, stride):
        return jnp.concatenate(
            [stage[i, pl.ds(start, size, stride=stride), :] for i in range(2)], axis=1
        )

    def pack_rims(k):
        for side, column in enumerate((0, W - 1)):
            for f in range(F):
                rim = staged(f * H * W + column, H, W)
                colpack[k, side, f] = rim.astype(BF16)
            for end, line_at in enumerate((0, H - 1)):
                cornerpack[k, end, side] = staged(line_at * W + column, F, H * W)

    def rim_copies(k, full, own, halo, turn):
        last = own + (F - 2 if turn > 0 else 0)
        inner = F - 2 if turn > 0 else 0
        moves = []
        for start, n in PIECES:
            src = full.at[pl.ds(last, 2), pl.ds(start, n)]
            moves.append(((turn, 0, 0), src, full.at[pl.ds(halo, 2), pl.ds(start, n)]))
        for step, src, dst in ((1, H, 0), (-1, 1, H + 1)):
            moves.append(((0, step, 0), full.at[pl.ds(own, F), src], full.at[pl.ds(own, F), dst]))
            moves.append(((turn, step, 0), full.at[pl.ds(last, 2), src], full.at[pl.ds(halo, 2), dst]))
        for step, src, dst in ((1, 1, 0), (-1, 0, 1)):
            moves.append(((0, 0, step), colpack.at[k, src], colhalo.at[k, dst, pl.ds(own, F)]))
            moves.append(
                ((turn, 0, step), colpack.at[k, src, pl.ds(inner, 2)], colhalo.at[k, dst, pl.ds(halo, 2)])
            )
        for down, over in itertools.product((1, -1), repeat=2):
            src = cornerpack.at[k, int(down > 0), int(over > 0)]
            place = (int(down < 0), int(over < 0))
            moves.append(((0, down, over), src, cornerhalo.at[k, 0, place[0], place[1]]))
            moves.append(((turn, down, over), src, cornerhalo.at[k, 1, place[0], place[1]]))
        copies = [
            pltpu.make_async_remote_copy(
                src_ref=src,
                dst_ref=dst,
                send_sem=halo_send.at[k, j],
                recv_sem=halo_recv.at[k, j],
                device_id=at(o),
                device_id_type=MESH,
            )
            for j, (o, src, dst) in enumerate(moves)
        ]
        packed = [j >= len(PIECES) + 4 for j in range(len(moves))]
        far = [o[0] != 0 for o, _, _ in moves]
        pick = lambda p, a: [x for x, y, z in zip(copies, packed, far) if y == p and z == a]
        return pick(False, False), pick(False, True), pick(True, False), pick(True, True)

    def start_all(*groups):
        for group in groups:
            for copy in group:
                copy.start()

    def await_rims(*groups):
        for group in groups:
            for copy in group:
                copy.wait_recv()

    def side_columns(ks, first, count, turn, change):
        other = int(count < F)
        skip = F - 2 if other and turn > 0 else 0
        for side in range(2):

            def one(f, carry, side=side):
                values = [colhalo[k, side, f].astype(F32) for k in ks]
                colside[side, f, pl.ds(1, H)] = change(f, *values)
                return carry

            lax.fori_loop(first, first + count, one, 0)
            for end, place in ((0, 0), (1, H + 1)):
                for f in range(count):
                    values = [cornerhalo[k, other, end, side, pl.ds(skip + f, 1)] for k in ks]
                    colside[side, first + f, pl.ds(place, 1)] = change(first + f, *values)

        @pl.when(c == 0)
        def _():
            colside[0, pl.ds(first, count)] = jnp.zeros((count,) + colside.shape[2:], F32)

        @pl.when(c == cols - 1)
        def _():
            colside[1, pl.ds(first, count)] = jnp.zeros((count,) + colside.shape[2:], F32)

    def build(full, first, count, edge, change):
        column = lax.broadcasted_iota(jnp.int32, (6, W, C), 1)

        def one(f, carry):
            for h in range(0, H + 2, 6):
                x = change(f, full[f, pl.ds(h, 6)].astype(F32))
                left = colside[0, f, pl.ds(h, 6)].reshape(6, 1, C)
                right = colside[1, f, pl.ds(h, 6)].reshape(6, 1, C)
                taps[1, f, pl.ds(h, 6)] = x.astype(BF16)
                taps[0, f, pl.ds(h, 6)] = jnp.where(
                    column == 0, left, pltpu.roll(x, 1, 1)
                ).astype(BF16)
                taps[2, f, pl.ds(h, 6)] = jnp.where(
                    column == W - 1, right, pltpu.roll(x, W - 1, 1)
                ).astype(BF16)
            return carry

        lax.fori_loop(first, first + count, one, 0)

        @pl.when(r == 0)
        def _():
            taps[:, pl.ds(first, count), 0] = jnp.zeros((3, count, W, C), BF16)

        @pl.when(r == rows - 1)
        def _():
            taps[:, pl.ds(first, count), H + 1] = jnp.zeros((3, count, W, C), BF16)

        if count < F:

            @pl.when(t == edge)
            def _():
                for f in range(count):
                    for dw in range(3):
                        taps[dw, first + f] = jnp.zeros((H + 2, W, C), BF16)

    def convolve(f, weights, back):
        left = jnp.concatenate(
            [
                taps[dw, pl.ds(f + dt, 2), pl.ds(dh, H)].reshape(2 * H * W, C)
                for dt, dh, dw in TAPS
            ],
            axis=1,
        )
        if back:
            right = jnp.concatenate([weights[26 - n] for n in range(27)], axis=1)
            return lax.dot_general(left, right, (((1,), (1,)), ((), ())), preferred_element_type=F32)
        return jnp.dot(left, weights[...].reshape(27 * C, C), preferred_element_type=F32)

    def row_of(ref, i):
        return ref[pl.ds(i, 1), :]

    def sums(x):
        return jnp.sum(x.reshape(-1, 8, C), axis=0)

    def norm_grad(values, d, mean, inverse, gain, offset):
        normed = (values - mean) * inverse
        pre = normed * gain + offset
        s = sigmoid(pre)
        e = d * s * (1.0 + pre * (1.0 - s)) * gain
        return e, sums(e), sums(e * normed)

    for load in loads[4:]:
        load.wait()
    vectors = [ref[...].reshape(1, C) for ref in (bias1, gain1, offset1, gain2, offset2)]
    bias1, gain1, offset1, gain2, offset2 = vectors

    loads[0].wait()

    def first_sums(f, carry):
        x = actf[f + 2, pl.ds(1, H)].astype(F32).reshape(H * W, C)
        put_stage(f * H * W, x)
        part[0, f] = sums(x)
        part[1, f] = sums(x * x)
        return carry

    lax.fori_loop(0, F, first_sums, 0)
    mine[0] = packed_sums()
    pl.semaphore_wait(barrier, len(everyone))
    plane_start(0)
    past = rim_copies(0, actf, 2, 0, 1)
    start_all(past[0], past[1][1:])
    pack_rims(0)
    start_all(past[2], past[3])
    loads[1].wait()
    fill_stage(cotf)
    pack_rims(1)
    line_start(0, plane_end(0))
    start_all(past[1][:1])
    future = rim_copies(1, cotf, 0, 4, -1)
    start_all(future[0], future[2])
    stat1[...] = first_end()
    start_all(future[1], future[3])

    def activate(f, x):
        shape = (1,) * (x.ndim - 1) + (C,)
        mean = row_of(stat1, f).reshape(shape)
        inverse = row_of(stat1, f + 8).reshape(shape)
        u = (x - mean) * inverse * gain1.reshape(shape) + offset1.reshape(shape)
        return u * sigmoid(u)

    await_rims(past[0], past[2])
    side_columns((0,), 2, F, 1, activate)
    build(actf, 2, F, 0, activate)
    loads[2].wait()

    def first_layer(i, carry):
        @pl.when(i == 1)
        def _():
            await_rims(past[1], past[3])
            side_columns((0,), 0, 2, 1, activate)
            build(actf, 0, 2, 0, activate)

        f = 2 - 2 * i
        hidden = convolve(f, w1, False)
        x = actf[pl.ds(f + 2, 2), pl.ds(1, H)].astype(F32).reshape(2 * H * W, C)
        y = (x + hidden + bias1).astype(BF16)
        layf[pl.ds(f, 2), pl.ds(1, H)] = y.reshape(2, H, W, C)
        y = y.astype(F32)
        for j in range(2):
            z = y[j * H * W : (j + 1) * H * W]
            part[0, f + j] = sums(z)
            part[1, f + j] = sums(z * z)
        return carry

    lax.fori_loop(0, F // 2, first_layer, 0)
    chip_start(1, packed_sums(), True)
    layer_rims = rim_copies(2, layf, 0, 4, -1)
    start_all(layer_rims[0], layer_rims[1])
    fill_stage(layf)
    pack_rims(2)
    start_all(layer_rims[2], layer_rims[3])

    await_rims(future[0], future[2])
    loads[3].wait()
    same = lambda f, x: x
    side_columns((1,), 0, F, -1, same)
    build(cotf, 0, F, tms - 1, same)

    def second_grad(i, carry):
        @pl.when(i == 1)
        def _():
            await_rims(future[1], future[3])
            side_columns((1,), 4, 2, -1, same)
            build(cotf, 4, 2, tms - 1, same)

        f = 2 * i
        grad[pl.ds(f, 2)] = convolve(f, w2, True).reshape(2, H, W, C)
        return carry

    lax.fori_loop(0, F // 2, second_grad, 0)
    stat2[...] = forward_end(1, 1)

    def second_norm(f, carry):
        mean, inverse = row_of(stat2, f), row_of(stat2, f + 8)
        a = b = jnp.zeros((8, C), F32)
        for h in range(0, H, 8):
            v = layf[f, pl.ds(h + 1, 8)].astype(F32).reshape(8 * W, C)
            d = grad[f, pl.ds(h, 8)].reshape(8 * W, C)
            e, da, db = norm_grad(v, d, mean, inverse, gain2, offset2)
            x = cotf[f, pl.ds(h + 1, 8)].astype(F32).reshape(8 * W, C) + inverse * e
            grad[f, pl.ds(h, 8)] = x.reshape(8, W, C)
            xf[f, pl.ds(h + 1, 8)] = x.astype(BF16).reshape(8, W, C)
            a, b = a + da, b + db
        part[0, f] = a
        part[1, f] = b
        return carry

    lax.fori_loop(0, F, second_norm, 0)
    chip_start(2, backward_terms(packed_sums(), 1), False)
    x_rims = rim_copies(3, xf, 0, 4, -1)
    start_all(x_rims[0], x_rims[1])
    fill_stage(xf)
    pack_rims(3)
    start_all(x_rims[2], x_rims[3])
    rest2[...] = backward_end(2)

    def settle(f, x, v):
        shape = (1,) * (x.ndim - 1) + (C,)
        r1 = row_of(rest2, f).reshape(shape)
        r2 = row_of(rest2, f + 8).reshape(shape)
        return x + (r1 + 2.0 * v * r2)

    def middle(f, carry):
        for h in range(0, H, 8):
            v = layf[f, pl.ds(h + 1, 8)].astype(F32)
            gmf[f, pl.ds(h + 1, 8)] = settle(f, grad[f, pl.ds(h, 8)], v).astype(BF16)
        return carry

    lax.fori_loop(0, F, middle, 0)

    def settle_rows(f, h, n):
        x, v = xf[f, pl.ds(h, n)].astype(F32), layf[f, pl.ds(h, n)].astype(F32)
        gmf[f, pl.ds(h, n)] = settle(f, x, v).astype(BF16)

    def middle_rows(f, carry):
        settle_rows(f, 0, 1)
        settle_rows(f, H + 1, 1)
        return carry

    def middle_frames(f, carry):
        for h in range(0, H + 2, 6):
            settle_rows(f, h, 6)
        return carry

    await_rims(layer_rims[0], layer_rims[2], x_rims[0], x_rims[2])
    lax.fori_loop(0, F, middle_rows, 0)
    side_columns((3, 2), 0, F, -1, settle)

    build(gmf, 0, F, tms - 1, same)

    def first_grad(i, carry):
        @pl.when(i == 1)
        def _():
            await_rims(layer_rims[1], layer_rims[3], x_rims[1], x_rims[3])
            lax.fori_loop(F, F + 2, middle_frames, 0)
            side_columns((3, 2), 4, 2, -1, settle)
            build(gmf, 4, 2, tms - 1, same)

        f = 2 * i
        grad[pl.ds(f, 2)] = convolve(f, w1, True).reshape(2, H, W, C)
        return carry

    lax.fori_loop(0, F // 2, first_grad, 0)

    def first_norm(f, carry):
        mean, inverse = row_of(stat1, f + 2), row_of(stat1, f + 10)
        a = b = jnp.zeros((8, C), F32)
        for h in range(0, H, 8):
            v = actf[f + 2, pl.ds(h + 1, 8)].astype(F32).reshape(8 * W, C)
            d = grad[f, pl.ds(h, 8)].reshape(8 * W, C)
            e, da, db = norm_grad(v, d, mean, inverse, gain1, offset1)
            grad[f, pl.ds(h, 8)] = e.reshape(8, W, C)
            a, b = a + da, b + db
        part[0, f] = a
        part[1, f] = b
        return carry

    lax.fori_loop(0, F, first_norm, 0)
    chip_start(3, backward_terms(packed_sums(), 0), False)
    rest1[...] = backward_end(3)

    def finish(f, carry):
        inverse = row_of(stat1, f + 10)
        r1, r2 = row_of(rest1, f), row_of(rest1, f + 8)
        for h in range(0, H, 8):
            v = actf[f + 2, pl.ds(h + 1, 8)].astype(F32).reshape(8 * W, C)
            e = grad[f, pl.ds(h, 8)].reshape(8 * W, C)
            x = gmf[f, pl.ds(h + 1, 8)].astype(F32).reshape(8 * W, C)
            y = x + (inverse * e + r1 + 2.0 * v * r2)
            out_ref[f, pl.ds(h, 8)] = y.astype(BF16).reshape(8, W, C)
        return carry

    lax.fori_loop(0, F, finish, 0)

    for group in past + future + layer_rims + x_rims:
        for copy in group:
            copy.wait_send()
    await_all(plane_in.at[0], plane_send.at[0])
    await_all(line_in.at[0], line_send.at[0])
    for k in range(1, 4):
        await_all(near_in.at[k], near_send.at[k])
        for a in steps:

            @pl.when(goes(a, k == 1))
            def _(a=a, k=k):
                await_all(far_in.at[k, a - 1], far_send.at[k, a - 1])


def solution(mesh):
    sizes = tuple(mesh.shape[a] for a in AXES)
    n_plane, n_line = sizes[1] * sizes[2] - 1, sizes[0] - 1
    n_chips = sizes[1] * sizes[2] // 2
    rims = 18
    full = (F + 2, H + 2, W, C)

    def step(act, cot, w1, b1, g1, o1, w2, g2, o2):
        hbm = pl.BlockSpec(memory_space=pltpu.HBM)
        operands = (act, cot, w1.reshape(27, C, C), w2.reshape(27, C, C), b1, g1, o1, g2, o2)
        operands = [pltpu.with_memory_space_constraint(x, pltpu.HBM) for x in operands]
        vmem = pl.BlockSpec(memory_space=pltpu.VMEM)
        return pl.pallas_call(
            functools.partial(kernel, sizes),
            name="vae_grad",
            out_shape=pltpu.VMEM((F, H, W, C), BF16),
            in_specs=[hbm] * 9,
            out_specs=vmem,
            scratch_shapes=[
                pltpu.VMEM(full, BF16),
                pltpu.VMEM(full, BF16),
                pltpu.VMEM(full, BF16),
                pltpu.VMEM((27, C, C), BF16),
                pltpu.VMEM((27, C, C), BF16),
                pltpu.VMEM((C,), F32),
                pltpu.VMEM((C,), F32),
                pltpu.VMEM((C,), F32),
                pltpu.VMEM((C,), F32),
                pltpu.VMEM((C,), F32),
                pltpu.VMEM((3,) + full, BF16),
                pltpu.VMEM((F, H, W, C), F32),
                pltpu.VMEM(full, BF16),
                pltpu.VMEM(full, BF16),
                pltpu.VMEM((2, F * H * W, 128), F32),
                pltpu.VMEM((4, 2, F, H, C), BF16),
                pltpu.VMEM((4, 2, 2, F, C), F32),
                pltpu.VMEM((4, 2, F + 2, H, C), BF16),
                pltpu.VMEM((4, 2, 2, 2, F, C), F32),
                pltpu.VMEM((2, F + 2, 24, C), F32),
                pltpu.VMEM((2, F, 8, C), F32),
                pltpu.VMEM((C, 128), BF16),
                pltpu.VMEM((128, C), BF16),
                pltpu.VMEM((16, C), F32),
                pltpu.VMEM((16, C), F32),
                pltpu.VMEM((16, C), F32),
                pltpu.VMEM((16, C), F32),
                pltpu.VMEM((2, 2, 128), F32),
                pltpu.VMEM((4, 2, 128), F32),
                pltpu.VMEM((4, 2, 128), F32),
                pltpu.VMEM((1, n_plane, 2, 128), F32),
                pltpu.VMEM((1, n_line, 2, 128), F32),
                pltpu.VMEM((4, 2, 128), F32),
                pltpu.VMEM((4, 1, 128), F32),
                pltpu.VMEM((4, 2, 128), F32),
                pltpu.VMEM((4, n_chips - 1, 2, 128), F32),
                pltpu.VMEM((4, n_line, n_chips, 1, 128), F32),
                pltpu.VMEM((n_line, 1, 128), F32),
                pltpu.SemaphoreType.DMA((9,)),
                pltpu.SemaphoreType.DMA((4, rims)),
                pltpu.SemaphoreType.DMA((4, rims)),
                *[pltpu.SemaphoreType.DMA((4,))] * 8,
                *[pltpu.SemaphoreType.DMA((4, n_line))] * 2,
            ],
            compiler_params=pltpu.CompilerParams(
                collective_id=0, has_side_effects=True, vmem_limit_bytes=62 << 20
            ),
        )(*operands)

    tile = P(*AXES, None)
    return jax.shard_map(
        step,
        mesh=mesh,
        in_specs=(tile, tile) + (P(),) * 7,
        out_specs=tile,
        check_vma=False,
    )
```

```python
import functools
import itertools

import jax
import jax.numpy as jnp
from jax import lax
from jax.experimental import pallas as pl
from jax.experimental.pallas import tpu as pltpu
from jax.sharding import PartitionSpec as P

MESH = pl.DeviceIdType.MESH
BF16, F32 = jnp.bfloat16, jnp.float32
EPS = 1e-6
F, H, W, C, G = 4, 16, 16, 256, 32
TAPS = tuple(itertools.product(range(3), repeat=3))
AXES = ("tm", "row", "col")
PIECES = ((1, 11), (12, 5))


def offsets_of(sizes):
    tms, rows, cols = sizes
    plane = [(0, b, d) for b in range(rows) for d in range(cols) if (b, d) != (0, 0)]
    plane.sort(key=lambda o: -(min(o[1], rows - o[1]) + min(o[2], cols - o[2])))
    line = [(a, 0, 0) for a in range(1, tms)]
    line.sort(key=lambda o: -min(o[0], tms - o[0]))
    rims = [
        (a % tms, b % rows, d % cols)
        for a in (-1, 1)
        for b in (-1, 0, 1)
        for d in (-1, 0, 1)
    ]
    everyone = list(dict.fromkeys(plane + line + rims))
    everyone.sort(key=lambda o: -sum(min(x, n - x) for x, n in zip(o, sizes)))
    chips = [
        (a, b, d)
        for a in range(tms)
        for b in range(rows)
        for d in range(0, cols, 2)
        if (a, b, d) != (0, 0, 0)
    ]
    chips.sort(
        key=lambda o: -2 * (min(o[0], tms - o[0]) + min(o[1], rows - o[1])) - min(o[2], cols - o[2])
    )
    return plane, line, everyone, chips


def sigmoid(u):
    return 0.5 * jnp.tanh(0.5 * u) + 0.5


def split3(x):
    high = x.astype(BF16)
    rest = x - high.astype(F32)
    middle = rest.astype(BF16)
    low = (rest - middle.astype(F32)).astype(BF16)
    return jnp.concatenate([high, middle, low], axis=0)


def exact_dot(x, picks):
    n = x.shape[0]
    y = jnp.dot(split3(x), picks, preferred_element_type=F32)
    return y[:n] + y[n : 2 * n] + y[2 * n :]


def frame_of_lane(shape):
    return lax.broadcasted_iota(jnp.int32, shape, len(shape) - 1) >> 5


def over_frames(x):
    return x + pltpu.roll(x, 32, 1) + pltpu.roll(x, 64, 1) + pltpu.roll(x, 96, 1)


def running(x):
    f = frame_of_lane(x.shape)
    return (
        x
        + jnp.where(f >= 1, pltpu.roll(x, 32, 1), 0.0)
        + jnp.where(f >= 2, pltpu.roll(x, 64, 1), 0.0)
        + jnp.where(f >= 3, pltpu.roll(x, 96, 1), 0.0)
    )


def running_back(x):
    f = frame_of_lane(x.shape)
    return (
        x
        + jnp.where(f <= 2, pltpu.roll(x, 96, 1), 0.0)
        + jnp.where(f <= 1, pltpu.roll(x, 64, 1), 0.0)
        + jnp.where(f <= 0, pltpu.roll(x, 32, 1), 0.0)
    )


def kernel(
    sizes,
    act_hbm,
    cot_hbm,
    w1_hbm,
    w2_hbm,
    bias1_hbm,
    gain1_hbm,
    offset1_hbm,
    gain2_hbm,
    offset2_hbm,
    out_ref,
    actf,
    cotf,
    gmf,
    w1,
    w2,
    bias1,
    gain1,
    offset1,
    gain2,
    offset2,
    taps,
    grad,
    layf,
    xf,
    xwide,
    stage,
    colpack,
    cornerpack,
    colhalo,
    cornerhalo,
    colside,
    part,
    gather_m,
    spread_m,
    stat1,
    stat2,
    rest1,
    rest2,
    ends,
    mine,
    line_mine,
    plane_in,
    line_in,
    chip_mine,
    chip_brief,
    pair_in,
    near_in,
    far_in,
    arrived,
    in_sem,
    halo_send,
    halo_recv,
    plane_send,
    plane_recv,
    line_send,
    line_recv,
    pair_send,
    pair_recv,
    near_send,
    near_recv,
    far_send,
    far_recv,
):
    tms, rows, cols = sizes
    t, r, c = (lax.axis_index(a) for a in AXES)
    plane, line, everyone, chips = offsets_of(sizes)
    plane_cells = float(H * rows * W * cols * (C // G))

    def at(o):
        return (
            lax.rem(t + (o[0] % tms), tms),
            lax.rem(r + (o[1] % rows), rows),
            lax.rem(c + (o[2] % cols), cols),
        )

    barrier = pltpu.get_barrier_semaphore()
    for o in everyone:
        pl.semaphore_signal(barrier, inc=1, device_id=at(o), device_id_type=MESH)

    loads = [
        pltpu.make_async_copy(act_hbm, actf.at[pl.ds(2, F), pl.ds(1, H)], in_sem.at[0]),
        pltpu.make_async_copy(cot_hbm, cotf.at[pl.ds(0, F), pl.ds(1, H)], in_sem.at[1]),
        pltpu.make_async_copy(w1_hbm, w1, in_sem.at[2]),
        pltpu.make_async_copy(w2_hbm, w2, in_sem.at[3]),
        pltpu.make_async_copy(bias1_hbm, bias1, in_sem.at[4]),
        pltpu.make_async_copy(gain1_hbm, gain1, in_sem.at[5]),
        pltpu.make_async_copy(offset1_hbm, offset1, in_sem.at[6]),
        pltpu.make_async_copy(gain2_hbm, gain2, in_sem.at[7]),
        pltpu.make_async_copy(offset2_hbm, offset2, in_sem.at[8]),
    ]
    for load in loads:
        load.start()

    channel = lax.broadcasted_iota(jnp.int32, (C, 128), 0) >> 3
    group = lax.broadcasted_iota(jnp.int32, (C, 128), 1) & (G - 1)
    gather_m[...] = jnp.where(channel == group, 1.0, 0.0).astype(BF16)
    channel = lax.broadcasted_iota(jnp.int32, (128, C), 1) >> 3
    group = lax.broadcasted_iota(jnp.int32, (128, C), 0) & (G - 1)
    spread_m[...] = jnp.where(channel == group, 1.0, 0.0).astype(BF16)

    def packed_sums():
        y = exact_dot(part[...].reshape(2 * F * 8, C), gather_m[...])
        y = y.reshape(2, F, 8, 128)
        f = frame_of_lane((2, 8, 128))
        z = jnp.zeros((2, 8, 128), F32)
        for i in range(F):
            z = z + jnp.where(f == i, y[:, i], 0.0)
        return jnp.sum(z, axis=1)

    def plane_copy(k, j):
        return pltpu.make_async_remote_copy(
            src_ref=mine.at[k],
            dst_ref=plane_in.at[k, j],
            send_sem=plane_send.at[k],
            recv_sem=plane_recv.at[k],
            device_id=at(plane[j]),
            device_id_type=MESH,
        )

    def line_copy(k, j):
        return pltpu.make_async_remote_copy(
            src_ref=line_mine.at[k],
            dst_ref=line_in.at[k, line[j][0] - 1],
            send_sem=line_send.at[k],
            recv_sem=line_recv.at[k],
            device_id=at(line[j]),
            device_id_type=MESH,
        )

    def await_all(buffer, sem):
        pltpu.make_async_copy(buffer, buffer, sem).wait()

    def plane_start(k):
        for j in range(len(plane)):
            plane_copy(k, j).start()

    def plane_end(k):
        await_all(plane_in.at[k], plane_recv.at[k])
        return mine[k] + jnp.sum(plane_in[k], axis=0)

    def line_start(k, value):
        line_mine[k] = value
        for j in range(len(line)):
            line_copy(k, j).start()

    def line_end(k):
        await_all(line_in.at[k], line_recv.at[k])
        return [line_in[k, j] for j in range(len(line))]

    def counts(first_frame):
        f = first_frame + frame_of_lane((1, 128)) + 1
        return jnp.maximum(f, 1).astype(F32) * plane_cells

    def moments(prefix, n):
        mean = prefix[0:1] / n
        return mean, lax.rsqrt(prefix[1:2] / n - mean * mean + EPS)

    def spread(first, second, before=None, after=None):
        row = lax.broadcasted_iota(jnp.int32, (8, 128), 0)
        f = frame_of_lane((8, 128))
        halves = []
        for i, own in enumerate((first, second)):
            own = jnp.broadcast_to(own, (8, 128))
            if before is not None:
                ahead = jnp.broadcast_to(before[i], (8, 128))
                frame = jnp.where(row < 2, row + 2, row - 2)
                own = jnp.where(row < 2, ahead, own)
            elif after is not None:
                behind = jnp.broadcast_to(after[i], (8, 128))
                frame = jnp.where(row < F, row, row - F)
                own = jnp.where(row < F, own, behind)
            else:
                frame = row
            halves.append(jnp.where(f == frame, own, 0.0))
        return exact_dot(jnp.concatenate(halves, axis=0), spread_m[...])

    def first_end():
        got = line_end(0)
        zero = jnp.zeros((2, 128), F32)
        near = jnp.where(t >= 1, got[0], zero)
        far = zero
        for j in range(1, len(line)):
            far = far + jnp.where(t >= j + 1, got[j], zero)
        own = moments(over_frames(far + near) + running(line_mine[0]), counts(t * F))
        ends[0, 0:1] = own[0]
        ends[0, 1:2] = own[1]
        before = moments(over_frames(far) + running(near), counts(t * F - F))
        return spread(own[0], own[1], before)

    def partner_copy(k):
        return pltpu.make_async_remote_copy(
            src_ref=mine.at[k],
            dst_ref=pair_in.at[k],
            send_sem=pair_send.at[k],
            recv_sem=pair_recv.at[k],
            device_id=(t, r, c + 1 - 2 * lax.rem(c, 2)),
            device_id_type=MESH,
        )

    def chip_copy(k, o):
        inside = o[0] == 0
        place = o[1] * (cols // 2) + o[2] // 2
        return pltpu.make_async_remote_copy(
            src_ref=chip_mine.at[k] if inside else chip_brief.at[k],
            dst_ref=near_in.at[k, place - 1] if inside else far_in.at[k, o[0] - 1, place],
            send_sem=near_send.at[k] if inside else far_send.at[k, o[0] - 1],
            recv_sem=near_recv.at[k] if inside else far_recv.at[k, o[0] - 1],
            device_id=at(o),
            device_id_type=MESH,
        )

    def goes(a, forward):
        return t + a < tms if forward else t + a >= tms

    def comes(a, forward):
        return t >= a if forward else t < a

    steps = sorted(range(1, tms), key=lambda a: -min(a, tms - a))

    def chip_start(k, value, forward):
        mine[k] = value
        pair = partner_copy(k)
        pair.start()
        pair.wait_recv()
        value = value + pair_in[k]
        chip_mine[k] = value
        f = frame_of_lane((1, 128))
        whole = over_frames(value)
        first = jnp.where(f == 2, pltpu.roll(value, 64, 1)[0:1], pltpu.roll(value, 96, 1)[1:2])
        both = jnp.where(f == 0, whole[0:1], whole[1:2])
        chip_brief[k] = jnp.where(f < 2, both, first)
        for a in steps:

            @pl.when(goes(a, forward))
            def _(a=a):
                for o in chips:
                    if o[0] == a:
                        chip_copy(k, o).start()

        for o in chips:
            if o[0] == 0:
                chip_copy(k, o).start()
        pair.wait_send()

    def chip_end(k, forward):
        arrived[...] = jnp.zeros(arrived.shape, F32)
        await_all(near_in.at[k], near_recv.at[k])
        own = chip_mine[k] + jnp.sum(near_in[k], axis=0)
        for a in reversed(steps):

            @pl.when(comes(a, forward))
            def _(a=a):
                await_all(far_in.at[k, a - 1], far_recv.at[k, a - 1])
                arrived[a - 1] = jnp.sum(far_in[k, a - 1], axis=0)

        return own, [arrived[a] for a in range(tms - 1)]

    def widen(x):
        f = frame_of_lane((1, 128))
        rows = [jnp.where(f == i, x, 0.0) for i in range(2)]
        return over_frames(jnp.concatenate(rows, axis=0))

    def forward_end(k, layer):
        own, got = chip_end(k, True)
        earlier = sum(got[1:], got[0])
        own = moments(widen(earlier) + running(own), counts(t * F))
        ends[layer, 0:1] = own[0]
        ends[layer, 1:2] = own[1]
        return spread(own[0], own[1])

    def backward_terms(totals, layer):
        mean, inverse = ends[layer, 0:1], ends[layer, 1:2]
        n = counts(t * F)
        a, b = totals[0:1], totals[1:2]
        first = (-inverse * a + b * inverse * inverse * mean) / n
        second = -0.5 * b * inverse * inverse / n
        return jnp.concatenate([first, second], axis=0)

    def backward_end(k):
        own, got = chip_end(k, False)
        near = got[-1]
        later = widen(sum(got[1:], got[0]))
        f = frame_of_lane((1, 128))
        first = jnp.concatenate([pltpu.roll(near, 96, 1), pltpu.roll(near, 64, 1)], axis=0)
        behind = later - jnp.where(f == 1, first, 0.0)
        rest = later + running_back(own)
        return spread(rest[0:1], rest[1:2], after=(behind[0:1], behind[1:2]))

    def put_stage(start, x):
        for i in range(2):
            stage[i, pl.ds(start, x.shape[0])] = x[:, i * 128 : i * 128 + 128]

    def fill_stage(full):
        def one(f, carry):
            put_stage(f * H * W, full[f, pl.ds(1, H)].astype(F32).reshape(H * W, C))
            return carry

        lax.fori_loop(0, F, one, 0)

    def staged(start, size, stride):
        return jnp.concatenate(
            [stage[i, pl.ds(start, size, stride=stride), :] for i in range(2)], axis=1
        )

    def pack_rims(k):
        for side, column in enumerate((0, W - 1)):
            for f in range(F):
                rim = staged(f * H * W + column, H, W)
                colpack[k, side, f] = rim.astype(BF16)
            for end, line_at in enumerate((0, H - 1)):
                cornerpack[k, end, side] = staged(line_at * W + column, F, H * W)

    def rim_copies(k, full, own, halo, turn):
        last = own + (F - 2 if turn > 0 else 0)
        inner = F - 2 if turn > 0 else 0
        moves = []
        for start, n in PIECES:
            src = full.at[pl.ds(last, 2), pl.ds(start, n)]
            moves.append(((turn, 0, 0), src, full.at[pl.ds(halo, 2), pl.ds(start, n)]))
        for step, src, dst in ((1, H, 0), (-1, 1, H + 1)):
            moves.append(((0, step, 0), full.at[pl.ds(own, F), src], full.at[pl.ds(own, F), dst]))
            moves.append(((turn, step, 0), full.at[pl.ds(last, 2), src], full.at[pl.ds(halo, 2), dst]))
        for step, src, dst in ((1, 1, 0), (-1, 0, 1)):
            moves.append(((0, 0, step), colpack.at[k, src], colhalo.at[k, dst, pl.ds(own, F)]))
            moves.append(
                ((turn, 0, step), colpack.at[k, src, pl.ds(inner, 2)], colhalo.at[k, dst, pl.ds(halo, 2)])
            )
        for down, over in itertools.product((1, -1), repeat=2):
            src = cornerpack.at[k, int(down > 0), int(over > 0)]
            place = (int(down < 0), int(over < 0))
            moves.append(((0, down, over), src, cornerhalo.at[k, 0, place[0], place[1]]))
            moves.append(((turn, down, over), src, cornerhalo.at[k, 1, place[0], place[1]]))
        copies = [
            pltpu.make_async_remote_copy(
                src_ref=src,
                dst_ref=dst,
                send_sem=halo_send.at[k, j],
                recv_sem=halo_recv.at[k, j],
                device_id=at(o),
                device_id_type=MESH,
            )
            for j, (o, src, dst) in enumerate(moves)
        ]
        packed = [j >= len(PIECES) + 4 for j in range(len(moves))]
        far = [o[0] != 0 for o, _, _ in moves]
        pick = lambda p, a: [x for x, y, z in zip(copies, packed, far) if y == p and z == a]
        return pick(False, False), pick(False, True), pick(True, False), pick(True, True)

    def start_all(*groups):
        for group in groups:
            for copy in group:
                copy.start()

    def await_rims(*groups):
        for group in groups:
            for copy in group:
                copy.wait_recv()

    def side_columns(ks, first, count, turn, change):
        other = int(count < F)
        skip = F - 2 if other and turn > 0 else 0
        for side in range(2):

            def one(f, carry, side=side):
                values = [colhalo[k, side, f].astype(F32) for k in ks]
                colside[side, f, pl.ds(1, H)] = change(f, *values)
                return carry

            lax.fori_loop(first, first + count, one, 0)
            for end, place in ((0, 0), (1, H + 1)):
                for f in range(count):
                    values = [cornerhalo[k, other, end, side, pl.ds(skip + f, 1)] for k in ks]
                    colside[side, first + f, pl.ds(place, 1)] = change(first + f, *values)

        @pl.when(c == 0)
        def _():
            colside[0, pl.ds(first, count)] = jnp.zeros((count,) + colside.shape[2:], F32)

        @pl.when(c == cols - 1)
        def _():
            colside[1, pl.ds(first, count)] = jnp.zeros((count,) + colside.shape[2:], F32)

    def build(get, first, count, edge):
        column = lax.broadcasted_iota(jnp.int32, (6, W, C), 1)

        def one(f, carry):
            for h in range(0, H + 2, 6):
                x = get(f, h)
                left = colside[0, f, pl.ds(h, 6)].reshape(6, 1, C)
                right = colside[1, f, pl.ds(h, 6)].reshape(6, 1, C)
                taps[1, f, pl.ds(h, 6)] = x.astype(BF16)
                taps[0, f, pl.ds(h, 6)] = jnp.where(
                    column == 0, left, pltpu.roll(x, 1, 1)
                ).astype(BF16)
                taps[2, f, pl.ds(h, 6)] = jnp.where(
                    column == W - 1, right, pltpu.roll(x, W - 1, 1)
                ).astype(BF16)
            return carry

        lax.fori_loop(first, first + count, one, 0)

        @pl.when(r == 0)
        def _():
            taps[:, pl.ds(first, count), 0] = jnp.zeros((3, count, W, C), BF16)

        @pl.when(r == rows - 1)
        def _():
            taps[:, pl.ds(first, count), H + 1] = jnp.zeros((3, count, W, C), BF16)

        if count < F:

            @pl.when(t == edge)
            def _():
                for f in range(count):
                    for dw in range(3):
                        taps[dw, first + f] = jnp.zeros((H + 2, W, C), BF16)

    def convolve(f, weights, back):
        left = jnp.concatenate(
            [
                taps[dw, pl.ds(f + dt, 2), pl.ds(dh, H)].reshape(2 * H * W, C)
                for dt, dh, dw in TAPS
            ],
            axis=1,
        )
        if back:
            right = jnp.concatenate([weights[26 - n] for n in range(27)], axis=1)
            return lax.dot_general(left, right, (((1,), (1,)), ((), ())), preferred_element_type=F32)
        return jnp.dot(left, weights[...].reshape(27 * C, C), preferred_element_type=F32)

    def row_of(ref, i):
        return ref[pl.ds(i, 1), :]

    def sums(x):
        return jnp.sum(x.reshape(-1, 8, C), axis=0)

    def norm_grad(values, d, mean, inverse, gain, offset):
        normed = (values - mean) * inverse
        pre = normed * gain + offset
        s = sigmoid(pre)
        e = d * s * (1.0 + pre * (1.0 - s)) * gain
        return e, sums(e), sums(e * normed)

    for load in loads[4:]:
        load.wait()
    vectors = [ref[...].reshape(1, C) for ref in (bias1, gain1, offset1, gain2, offset2)]
    bias1, gain1, offset1, gain2, offset2 = vectors

    loads[0].wait()

    def first_sums(f, carry):
        x = actf[f + 2, pl.ds(1, H)].astype(F32).reshape(H * W, C)
        put_stage(f * H * W, x)
        part[0, f] = sums(x)
        part[1, f] = sums(x * x)
        return carry

    lax.fori_loop(0, F, first_sums, 0)
    mine[0] = packed_sums()
    pl.semaphore_wait(barrier, len(everyone))
    plane_start(0)
    past = rim_copies(0, actf, 2, 0, 1)
    start_all(past[0], past[1][1:])
    pack_rims(0)
    start_all(past[2], past[3])
    loads[1].wait()
    fill_stage(cotf)
    pack_rims(1)
    line_start(0, plane_end(0))
    start_all(past[1][:1])
    future = rim_copies(1, cotf, 0, 4, -1)
    start_all(future[0], future[2])
    stat1[...] = first_end()
    start_all(future[1], future[3])

    def activate(f, x):
        shape = (1,) * (x.ndim - 1) + (C,)
        mean = row_of(stat1, f).reshape(shape)
        inverse = row_of(stat1, f + 8).reshape(shape)
        u = (x - mean) * inverse * gain1.reshape(shape) + offset1.reshape(shape)
        return u * sigmoid(u)

    await_rims(past[0], past[2])
    side_columns((0,), 2, F, 1, activate)
    active_rows = lambda f, h: activate(f, actf[f, pl.ds(h, 6)].astype(F32))
    build(active_rows, 2, F, 0)
    loads[2].wait()

    def first_layer(i, carry):
        @pl.when(i == 1)
        def _():
            await_rims(past[1], past[3])
            side_columns((0,), 0, 2, 1, activate)
            build(active_rows, 0, 2, 0)

        f = 2 - 2 * i
        hidden = convolve(f, w1, False)
        x = actf[pl.ds(f + 2, 2), pl.ds(1, H)].astype(F32).reshape(2 * H * W, C)
        y = (x + hidden + bias1).astype(BF16)
        layf[pl.ds(f, 2), pl.ds(1, H)] = y.reshape(2, H, W, C)
        y = y.astype(F32)
        for j in range(2):
            z = y[j * H * W : (j + 1) * H * W]
            part[0, f + j] = sums(z)
            part[1, f + j] = sums(z * z)
        return carry

    lax.fori_loop(0, F // 2, first_layer, 0)
    chip_start(1, packed_sums(), True)
    layer_rims = rim_copies(2, layf, 0, 4, -1)
    start_all(layer_rims[0], layer_rims[1])
    fill_stage(layf)
    pack_rims(2)
    start_all(layer_rims[2], layer_rims[3])

    await_rims(future[0], future[2])
    loads[3].wait()
    same = lambda f, x: x
    side_columns((1,), 0, F, -1, same)
    cot_rows = lambda f, h: cotf[f, pl.ds(h, 6)].astype(F32)
    build(cot_rows, 0, F, tms - 1)

    def second_grad(i, carry):
        @pl.when(i == 1)
        def _():
            await_rims(future[1], future[3])
            side_columns((1,), 4, 2, -1, same)
            build(cot_rows, 4, 2, tms - 1)

        f = 2 * i
        grad[pl.ds(f, 2)] = convolve(f, w2, True).reshape(2, H, W, C)
        return carry

    lax.fori_loop(0, F // 2, second_grad, 0)
    stat2[...] = forward_end(1, 1)

    def second_norm(f, carry):
        mean, inverse = row_of(stat2, f), row_of(stat2, f + 8)
        a = b = jnp.zeros((8, C), F32)
        for h in range(0, H, 8):
            v = layf[f, pl.ds(h + 1, 8)].astype(F32).reshape(8 * W, C)
            d = grad[f, pl.ds(h, 8)].reshape(8 * W, C)
            e, da, db = norm_grad(v, d, mean, inverse, gain2, offset2)
            x = cotf[f, pl.ds(h + 1, 8)].astype(F32).reshape(8 * W, C) + inverse * e
            xwide[f, pl.ds(h + 1, 8)] = x.reshape(8, W, C)
            xf[f, pl.ds(h + 1, 8)] = x.astype(BF16).reshape(8, W, C)
            a, b = a + da, b + db
        part[0, f] = a
        part[1, f] = b
        return carry

    lax.fori_loop(0, 2, second_norm, 0)
    x_rims = rim_copies(3, xf, 0, 4, -1)
    start_all(x_rims[1][1:])
    lax.fori_loop(2, F, second_norm, 0)
    chip_start(2, backward_terms(packed_sums(), 1), False)
    start_all(x_rims[0], x_rims[1][:1])
    fill_stage(xf)
    pack_rims(3)
    start_all(x_rims[2], x_rims[3])
    await_rims(layer_rims[0], layer_rims[2], x_rims[0], x_rims[2])

    def widen_rows(f, carry):
        for h in (0, H + 1):
            xwide[f, h] = xf[f, h].astype(F32)
        return carry

    lax.fori_loop(0, F, widen_rows, 0)
    rest2[...] = backward_end(2)

    def settle(f, x, v):
        shape = (1,) * (x.ndim - 1) + (C,)
        r1 = row_of(rest2, f).reshape(shape)
        r2 = row_of(rest2, f + 8).reshape(shape)
        return x + (r1 + 2.0 * v * r2)

    def middle_rows(x):
        def get(f, h):
            g = settle(f, x[f, pl.ds(h, 6)].astype(F32), layf[f, pl.ds(h, 6)].astype(F32)).astype(BF16)
            gmf[f, pl.ds(h, 6)] = g
            return g.astype(F32)

        return get

    side_columns((3, 2), 0, F, -1, settle)
    build(middle_rows(xwide), 0, F, tms - 1)

    def first_grad(i, carry):
        @pl.when(i == 1)
        def _():
            await_rims(layer_rims[1], layer_rims[3], x_rims[1], x_rims[3])
            side_columns((3, 2), 4, 2, -1, settle)
            build(middle_rows(xf), 4, 2, tms - 1)

        both = convolve(2 * i, w1, True)
        for j in range(2):
            f = 2 * i + j
            mean, inverse = row_of(stat1, f + 2), row_of(stat1, f + 10)
            a = b = jnp.zeros((8, C), F32)
            for h in range(0, H, 8):
                v = actf[f + 2, pl.ds(h + 1, 8)].astype(F32).reshape(8 * W, C)
                d = both[(j * H + h) * W : (j * H + h + 8) * W]
                e, da, db = norm_grad(v, d, mean, inverse, gain1, offset1)
                x = gmf[f, pl.ds(h + 1, 8)].astype(F32).reshape(8 * W, C) + inverse * e
                grad[f, pl.ds(h, 8)] = x.reshape(8, W, C)
                a, b = a + da, b + db
            part[0, f] = a
            part[1, f] = b
        return carry

    lax.fori_loop(0, F // 2, first_grad, 0)
    chip_start(3, backward_terms(packed_sums(), 0), False)
    rest1[...] = backward_end(3)

    def finish(f, carry):
        r1, r2 = row_of(rest1, f), row_of(rest1, f + 8)
        for h in range(0, H, 8):
            v = actf[f + 2, pl.ds(h + 1, 8)].astype(F32).reshape(8 * W, C)
            y = grad[f, pl.ds(h, 8)].reshape(8 * W, C) + (r1 + 2.0 * v * r2)
            out_ref[f, pl.ds(h, 8)] = y.astype(BF16).reshape(8, W, C)
        return carry

    lax.fori_loop(0, F, finish, 0)

    for group in past + future + layer_rims + x_rims:
        for copy in group:
            copy.wait_send()
    await_all(plane_in.at[0], plane_send.at[0])
    await_all(line_in.at[0], line_send.at[0])
    for k in range(1, 4):
        await_all(near_in.at[k], near_send.at[k])
        for a in steps:

            @pl.when(goes(a, k == 1))
            def _(a=a, k=k):
                await_all(far_in.at[k, a - 1], far_send.at[k, a - 1])


def solution(mesh):
    sizes = tuple(mesh.shape[a] for a in AXES)
    n_plane, n_line = sizes[1] * sizes[2] - 1, sizes[0] - 1
    n_chips = sizes[1] * sizes[2] // 2
    rims = 18
    full = (F + 2, H + 2, W, C)

    def step(act, cot, w1, b1, g1, o1, w2, g2, o2):
        hbm = pl.BlockSpec(memory_space=pltpu.HBM)
        operands = (act, cot, w1.reshape(27, C, C), w2.reshape(27, C, C), b1, g1, o1, g2, o2)
        operands = [pltpu.with_memory_space_constraint(x, pltpu.HBM) for x in operands]
        vmem = pl.BlockSpec(memory_space=pltpu.VMEM)
        return pl.pallas_call(
            functools.partial(kernel, sizes),
            name="vae_grad",
            out_shape=pltpu.VMEM((F, H, W, C), BF16),
            in_specs=[hbm] * 9,
            out_specs=vmem,
            scratch_shapes=[
                pltpu.VMEM(full, BF16),
                pltpu.VMEM(full, BF16),
                pltpu.VMEM(full, BF16),
                pltpu.VMEM((27, C, C), BF16),
                pltpu.VMEM((27, C, C), BF16),
                pltpu.VMEM((C,), F32),
                pltpu.VMEM((C,), F32),
                pltpu.VMEM((C,), F32),
                pltpu.VMEM((C,), F32),
                pltpu.VMEM((C,), F32),
                pltpu.VMEM((3,) + full, BF16),
                pltpu.VMEM((F, H, W, C), F32),
                pltpu.VMEM(full, BF16),
                pltpu.VMEM(full, BF16),
                pltpu.VMEM(full, F32),
                pltpu.VMEM((2, F * H * W, 128), F32),
                pltpu.VMEM((4, 2, F, H, C), BF16),
                pltpu.VMEM((4, 2, 2, F, C), F32),
                pltpu.VMEM((4, 2, F + 2, H, C), BF16),
                pltpu.VMEM((4, 2, 2, 2, F, C), F32),
                pltpu.VMEM((2, F + 2, 24, C), F32),
                pltpu.VMEM((2, F, 8, C), F32),
                pltpu.VMEM((C, 128), BF16),
                pltpu.VMEM((128, C), BF16),
                pltpu.VMEM((16, C), F32),
                pltpu.VMEM((16, C), F32),
                pltpu.VMEM((16, C), F32),
                pltpu.VMEM((16, C), F32),
                pltpu.VMEM((2, 2, 128), F32),
                pltpu.VMEM((4, 2, 128), F32),
                pltpu.VMEM((4, 2, 128), F32),
                pltpu.VMEM((1, n_plane, 2, 128), F32),
                pltpu.VMEM((1, n_line, 2, 128), F32),
                pltpu.VMEM((4, 2, 128), F32),
                pltpu.VMEM((4, 1, 128), F32),
                pltpu.VMEM((4, 2, 128), F32),
                pltpu.VMEM((4, n_chips - 1, 2, 128), F32),
                pltpu.VMEM((4, n_line, n_chips, 1, 128), F32),
                pltpu.VMEM((n_line, 1, 128), F32),
                pltpu.SemaphoreType.DMA((9,)),
                pltpu.SemaphoreType.DMA((4, rims)),
                pltpu.SemaphoreType.DMA((4, rims)),
                *[pltpu.SemaphoreType.DMA((4,))] * 8,
                *[pltpu.SemaphoreType.DMA((4, n_line))] * 2,
            ],
            compiler_params=pltpu.CompilerParams(
                collective_id=0, has_side_effects=True, vmem_limit_bytes=62 << 20
            ),
        )(*operands)

    tile = P(*AXES, None)
    return jax.shard_map(
        step,
        mesh=mesh,
        in_specs=(tile, tile) + (P(),) * 7,
        out_specs=tile,
        check_vma=False,
    )
```

```python
import functools
import itertools

import jax
import jax.numpy as jnp
from jax import lax
from jax.experimental import pallas as pl
from jax.experimental.pallas import tpu as pltpu
from jax.sharding import PartitionSpec as P

MESH = pl.DeviceIdType.MESH
BF16, F32 = jnp.bfloat16, jnp.float32
EPS = 1e-6
F, H, W, C, G = 4, 16, 16, 256, 32
TAPS = tuple(itertools.product(range(3), repeat=3))
AXES = ("tm", "row", "col")
PIECES = ((1, 13), (14, 3))


def offsets_of(sizes):
    tms, rows, cols = sizes
    plane = [(0, b, d) for b in range(rows) for d in range(cols) if (b, d) != (0, 0)]
    plane.sort(key=lambda o: -(min(o[1], rows - o[1]) + min(o[2], cols - o[2])))
    line = [(a, 0, 0) for a in range(1, tms)]
    line.sort(key=lambda o: -min(o[0], tms - o[0]))
    rims = [
        (a % tms, b % rows, d % cols)
        for a in (-1, 1)
        for b in (-1, 0, 1)
        for d in (-1, 0, 1)
    ]
    everyone = list(dict.fromkeys(plane + line + rims))
    everyone.sort(key=lambda o: -sum(min(x, n - x) for x, n in zip(o, sizes)))
    chips = [
        (a, b, d)
        for a in range(tms)
        for b in range(rows)
        for d in range(0, cols, 2)
        if (a, b, d) != (0, 0, 0)
    ]
    chips.sort(
        key=lambda o: -2 * (min(o[0], tms - o[0]) + min(o[1], rows - o[1])) - min(o[2], cols - o[2])
    )
    return plane, line, everyone, chips


def sigmoid(u):
    return 0.5 * jnp.tanh(0.5 * u) + 0.5


def split3(x):
    high = x.astype(BF16)
    rest = x - high.astype(F32)
    middle = rest.astype(BF16)
    low = (rest - middle.astype(F32)).astype(BF16)
    return jnp.concatenate([high, middle, low], axis=0)


def exact_dot(x, picks):
    n = x.shape[0]
    y = jnp.dot(split3(x), picks, preferred_element_type=F32)
    return y[:n] + y[n : 2 * n] + y[2 * n :]


def frame_of_lane(shape):
    return lax.broadcasted_iota(jnp.int32, shape, len(shape) - 1) >> 5


def over_frames(x):
    return x + pltpu.roll(x, 32, 1) + pltpu.roll(x, 64, 1) + pltpu.roll(x, 96, 1)


def running(x):
    f = frame_of_lane(x.shape)
    return (
        x
        + jnp.where(f >= 1, pltpu.roll(x, 32, 1), 0.0)
        + jnp.where(f >= 2, pltpu.roll(x, 64, 1), 0.0)
        + jnp.where(f >= 3, pltpu.roll(x, 96, 1), 0.0)
    )


def running_back(x):
    f = frame_of_lane(x.shape)
    return (
        x
        + jnp.where(f <= 2, pltpu.roll(x, 96, 1), 0.0)
        + jnp.where(f <= 1, pltpu.roll(x, 64, 1), 0.0)
        + jnp.where(f <= 0, pltpu.roll(x, 32, 1), 0.0)
    )


def kernel(
    sizes,
    act_hbm,
    cot_hbm,
    w1_hbm,
    w2_hbm,
    bias1_hbm,
    gain1_hbm,
    offset1_hbm,
    gain2_hbm,
    offset2_hbm,
    out_ref,
    actf,
    cotf,
    gmf,
    w1,
    w2,
    bias1,
    gain1,
    offset1,
    gain2,
    offset2,
    taps,
    grad,
    layf,
    xf,
    xwide,
    stage,
    colpack,
    cornerpack,
    colhalo,
    cornerhalo,
    colside,
    part,
    gather_m,
    spread_m,
    stat1,
    stat2,
    rest1,
    rest2,
    ends,
    mine,
    line_mine,
    plane_in,
    line_in,
    chip_mine,
    chip_brief,
    pair_in,
    near_in,
    far_in,
    arrived,
    in_sem,
    halo_send,
    halo_recv,
    plane_send,
    plane_recv,
    line_send,
    line_recv,
    pair_send,
    pair_recv,
    near_send,
    near_recv,
    far_send,
    far_recv,
):
    tms, rows, cols = sizes
    t, r, c = (lax.axis_index(a) for a in AXES)
    plane, line, everyone, chips = offsets_of(sizes)
    plane_cells = float(H * rows * W * cols * (C // G))

    def at(o):
        return (
            lax.rem(t + (o[0] % tms), tms),
            lax.rem(r + (o[1] % rows), rows),
            lax.rem(c + (o[2] % cols), cols),
        )

    barrier = pltpu.get_barrier_semaphore()
    for o in everyone:
        pl.semaphore_signal(barrier, inc=1, device_id=at(o), device_id_type=MESH)

    loads = [
        pltpu.make_async_copy(act_hbm, actf.at[pl.ds(2, F), pl.ds(1, H)], in_sem.at[0]),
        pltpu.make_async_copy(cot_hbm, cotf.at[pl.ds(0, F), pl.ds(1, H)], in_sem.at[1]),
        pltpu.make_async_copy(w1_hbm, w1, in_sem.at[2]),
        pltpu.make_async_copy(w2_hbm, w2, in_sem.at[3]),
        pltpu.make_async_copy(bias1_hbm, bias1, in_sem.at[4]),
        pltpu.make_async_copy(gain1_hbm, gain1, in_sem.at[5]),
        pltpu.make_async_copy(offset1_hbm, offset1, in_sem.at[6]),
        pltpu.make_async_copy(gain2_hbm, gain2, in_sem.at[7]),
        pltpu.make_async_copy(offset2_hbm, offset2, in_sem.at[8]),
    ]
    for load in loads:
        load.start()

    channel = lax.broadcasted_iota(jnp.int32, (C, 128), 0) >> 3
    group = lax.broadcasted_iota(jnp.int32, (C, 128), 1) & (G - 1)
    gather_m[...] = jnp.where(channel == group, 1.0, 0.0).astype(BF16)
    channel = lax.broadcasted_iota(jnp.int32, (128, C), 1) >> 3
    group = lax.broadcasted_iota(jnp.int32, (128, C), 0) & (G - 1)
    spread_m[...] = jnp.where(channel == group, 1.0, 0.0).astype(BF16)

    def packed_sums():
        y = exact_dot(part[...].reshape(2 * F * 8, C), gather_m[...])
        y = y.reshape(2, F, 8, 128)
        f = frame_of_lane((2, 8, 128))
        z = jnp.zeros((2, 8, 128), F32)
        for i in range(F):
            z = z + jnp.where(f == i, y[:, i], 0.0)
        return jnp.sum(z, axis=1)

    def plane_copy(k, j):
        return pltpu.make_async_remote_copy(
            src_ref=mine.at[k],
            dst_ref=plane_in.at[k, j],
            send_sem=plane_send.at[k],
            recv_sem=plane_recv.at[k],
            device_id=at(plane[j]),
            device_id_type=MESH,
        )

    def line_copy(k, j):
        return pltpu.make_async_remote_copy(
            src_ref=line_mine.at[k],
            dst_ref=line_in.at[k, line[j][0] - 1],
            send_sem=line_send.at[k],
            recv_sem=line_recv.at[k],
            device_id=at(line[j]),
            device_id_type=MESH,
        )

    def await_all(buffer, sem):
        pltpu.make_async_copy(buffer, buffer, sem).wait()

    def plane_start(k):
        for j in range(len(plane)):
            plane_copy(k, j).start()

    def plane_end(k):
        await_all(plane_in.at[k], plane_recv.at[k])
        return mine[k] + jnp.sum(plane_in[k], axis=0)

    def line_start(k, value):
        line_mine[k] = value
        for j in range(len(line)):
            line_copy(k, j).start()

    def line_end(k):
        await_all(line_in.at[k], line_recv.at[k])
        return [line_in[k, j] for j in range(len(line))]

    def counts(first_frame):
        f = first_frame + frame_of_lane((1, 128)) + 1
        return jnp.maximum(f, 1).astype(F32) * plane_cells

    def moments(prefix, n):
        mean = prefix[0:1] / n
        return mean, lax.rsqrt(prefix[1:2] / n - mean * mean + EPS)

    def spread(first, second, before=None, after=None):
        row = lax.broadcasted_iota(jnp.int32, (8, 128), 0)
        f = frame_of_lane((8, 128))
        halves = []
        for i, own in enumerate((first, second)):
            own = jnp.broadcast_to(own, (8, 128))
            if before is not None:
                ahead = jnp.broadcast_to(before[i], (8, 128))
                frame = jnp.where(row < 2, row + 2, row - 2)
                own = jnp.where(row < 2, ahead, own)
            elif after is not None:
                behind = jnp.broadcast_to(after[i], (8, 128))
                frame = jnp.where(row < F, row, row - F)
                own = jnp.where(row < F, own, behind)
            else:
                frame = row
            halves.append(jnp.where(f == frame, own, 0.0))
        return exact_dot(jnp.concatenate(halves, axis=0), spread_m[...])

    def first_end():
        got = line_end(0)
        zero = jnp.zeros((2, 128), F32)
        near = jnp.where(t >= 1, got[0], zero)
        far = zero
        for j in range(1, len(line)):
            far = far + jnp.where(t >= j + 1, got[j], zero)
        own = moments(over_frames(far + near) + running(line_mine[0]), counts(t * F))
        ends[0, 0:1] = own[0]
        ends[0, 1:2] = own[1]
        before = moments(over_frames(far) + running(near), counts(t * F - F))
        return spread(own[0], own[1], before)

    def partner_copy(k):
        return pltpu.make_async_remote_copy(
            src_ref=mine.at[k],
            dst_ref=pair_in.at[k],
            send_sem=pair_send.at[k],
            recv_sem=pair_recv.at[k],
            device_id=(t, r, c + 1 - 2 * lax.rem(c, 2)),
            device_id_type=MESH,
        )

    def chip_copy(k, o):
        inside = o[0] == 0
        place = o[1] * (cols // 2) + o[2] // 2
        return pltpu.make_async_remote_copy(
            src_ref=chip_mine.at[k] if inside else chip_brief.at[k],
            dst_ref=near_in.at[k, place - 1] if inside else far_in.at[k, o[0] - 1, place],
            send_sem=near_send.at[k] if inside else far_send.at[k, o[0] - 1],
            recv_sem=near_recv.at[k] if inside else far_recv.at[k, o[0] - 1],
            device_id=at(o),
            device_id_type=MESH,
        )

    def goes(a, forward):
        return t + a < tms if forward else t + a >= tms

    def comes(a, forward):
        return t >= a if forward else t < a

    steps = sorted(range(1, tms), key=lambda a: -min(a, tms - a))

    def chip_start(k, value, forward):
        mine[k] = value
        pair = partner_copy(k)
        pair.start()
        pair.wait_recv()
        value = value + pair_in[k]
        chip_mine[k] = value
        f = frame_of_lane((1, 128))
        whole = over_frames(value)
        first = jnp.where(f == 2, pltpu.roll(value, 64, 1)[0:1], pltpu.roll(value, 96, 1)[1:2])
        both = jnp.where(f == 0, whole[0:1], whole[1:2])
        chip_brief[k] = jnp.where(f < 2, both, first)
        for a in steps:

            @pl.when(goes(a, forward))
            def _(a=a):
                for o in chips:
                    if o[0] == a:
                        chip_copy(k, o).start()

        for o in chips:
            if o[0] == 0:
                chip_copy(k, o).start()
        pair.wait_send()

    def chip_end(k, forward):
        arrived[...] = jnp.zeros(arrived.shape, F32)
        await_all(near_in.at[k], near_recv.at[k])
        own = chip_mine[k] + jnp.sum(near_in[k], axis=0)
        for a in reversed(steps):

            @pl.when(comes(a, forward))
            def _(a=a):
                await_all(far_in.at[k, a - 1], far_recv.at[k, a - 1])
                arrived[a - 1] = jnp.sum(far_in[k, a - 1], axis=0)

        return own, [arrived[a] for a in range(tms - 1)]

    def widen(x):
        f = frame_of_lane((1, 128))
        rows = [jnp.where(f == i, x, 0.0) for i in range(2)]
        return over_frames(jnp.concatenate(rows, axis=0))

    def forward_end(k, layer):
        own, got = chip_end(k, True)
        earlier = sum(got[1:], got[0])
        own = moments(widen(earlier) + running(own), counts(t * F))
        ends[layer, 0:1] = own[0]
        ends[layer, 1:2] = own[1]
        return spread(own[0], own[1])

    def backward_terms(totals, layer):
        mean, inverse = ends[layer, 0:1], ends[layer, 1:2]
        n = counts(t * F)
        a, b = totals[0:1], totals[1:2]
        first = (-inverse * a + b * inverse * inverse * mean) / n
        second = -0.5 * b * inverse * inverse / n
        return jnp.concatenate([first, second], axis=0)

    def backward_end(k):
        own, got = chip_end(k, False)
        near = got[-1]
        later = widen(sum(got[1:], got[0]))
        f = frame_of_lane((1, 128))
        first = jnp.concatenate([pltpu.roll(near, 96, 1), pltpu.roll(near, 64, 1)], axis=0)
        behind = later - jnp.where(f == 1, first, 0.0)
        rest = later + running_back(own)
        return spread(rest[0:1], rest[1:2], after=(behind[0:1], behind[1:2]))

    def put_stage(start, x):
        for i in range(2):
            stage[i, pl.ds(start, x.shape[0])] = x[:, i * 128 : i * 128 + 128]

    def fill_stage(full):
        def one(f, carry):
            put_stage(f * H * W, full[f, pl.ds(1, H)].astype(F32).reshape(H * W, C))
            return carry

        lax.fori_loop(0, F, one, 0)

    def staged(start, size, stride):
        return jnp.concatenate(
            [stage[i, pl.ds(start, size, stride=stride), :] for i in range(2)], axis=1
        )

    def pack_rims(k):
        for side, column in enumerate((0, W - 1)):
            for f in range(F):
                rim = staged(f * H * W + column, H, W)
                colpack[k, side, f] = rim.astype(BF16)
            for end, line_at in enumerate((0, H - 1)):
                cornerpack[k, end, side] = staged(line_at * W + column, F, H * W)

    def rim_copies(k, full, own, halo, turn):
        last = own + (F - 2 if turn > 0 else 0)
        inner = F - 2 if turn > 0 else 0
        moves = []
        for start, n in PIECES:
            src = full.at[pl.ds(last, 2), pl.ds(start, n)]
            moves.append(((turn, 0, 0), src, full.at[pl.ds(halo, 2), pl.ds(start, n)]))
        for step, src, dst in ((1, H, 0), (-1, 1, H + 1)):
            moves.append(((0, step, 0), full.at[pl.ds(own, F), src], full.at[pl.ds(own, F), dst]))
            moves.append(((turn, step, 0), full.at[pl.ds(last, 2), src], full.at[pl.ds(halo, 2), dst]))
        for step, src, dst in ((1, 1, 0), (-1, 0, 1)):
            moves.append(((0, 0, step), colpack.at[k, src], colhalo.at[k, dst, pl.ds(own, F)]))
            moves.append(
                ((turn, 0, step), colpack.at[k, src, pl.ds(inner, 2)], colhalo.at[k, dst, pl.ds(halo, 2)])
            )
        for down, over in itertools.product((1, -1), repeat=2):
            src = cornerpack.at[k, int(down > 0), int(over > 0)]
            place = (int(down < 0), int(over < 0))
            moves.append(((0, down, over), src, cornerhalo.at[k, 0, place[0], place[1]]))
            moves.append(((turn, down, over), src, cornerhalo.at[k, 1, place[0], place[1]]))
        copies = [
            pltpu.make_async_remote_copy(
                src_ref=src,
                dst_ref=dst,
                send_sem=halo_send.at[k, j],
                recv_sem=halo_recv.at[k, j],
                device_id=at(o),
                device_id_type=MESH,
            )
            for j, (o, src, dst) in enumerate(moves)
        ]
        packed = [j >= len(PIECES) + 4 for j in range(len(moves))]
        far = [o[0] != 0 for o, _, _ in moves]
        pick = lambda p, a: [x for x, y, z in zip(copies, packed, far) if y == p and z == a]
        return pick(False, False), pick(False, True), pick(True, False), pick(True, True)

    def start_all(*groups):
        for group in groups:
            for copy in group:
                copy.start()

    def await_rims(*groups):
        for group in groups:
            for copy in group:
                copy.wait_recv()

    def side_columns(ks, first, count, turn, change):
        other = int(count < F)
        skip = F - 2 if other and turn > 0 else 0
        for side in range(2):

            def one(f, carry, side=side):
                values = [colhalo[k, side, f].astype(F32) for k in ks]
                colside[side, f, pl.ds(1, H)] = change(f, *values)
                return carry

            lax.fori_loop(first, first + count, one, 0)
            for end, place in ((0, 0), (1, H + 1)):
                for f in range(count):
                    values = [cornerhalo[k, other, end, side, pl.ds(skip + f, 1)] for k in ks]
                    colside[side, first + f, pl.ds(place, 1)] = change(first + f, *values)

        @pl.when(c == 0)
        def _():
            colside[0, pl.ds(first, count)] = jnp.zeros((count,) + colside.shape[2:], F32)

        @pl.when(c == cols - 1)
        def _():
            colside[1, pl.ds(first, count)] = jnp.zeros((count,) + colside.shape[2:], F32)

    def build(get, first, count, edge):
        column = lax.broadcasted_iota(jnp.int32, (6, W, C), 1)

        def one(f, carry):
            for h in range(0, H + 2, 6):
                x = get(f, h)
                left = colside[0, f, pl.ds(h, 6)].reshape(6, 1, C)
                right = colside[1, f, pl.ds(h, 6)].reshape(6, 1, C)
                taps[1, f, pl.ds(h, 6)] = x.astype(BF16)
                taps[0, f, pl.ds(h, 6)] = jnp.where(
                    column == 0, left, pltpu.roll(x, 1, 1)
                ).astype(BF16)
                taps[2, f, pl.ds(h, 6)] = jnp.where(
                    column == W - 1, right, pltpu.roll(x, W - 1, 1)
                ).astype(BF16)
            return carry

        lax.fori_loop(first, first + count, one, 0)

        @pl.when(r == 0)
        def _():
            taps[:, pl.ds(first, count), 0] = jnp.zeros((3, count, W, C), BF16)

        @pl.when(r == rows - 1)
        def _():
            taps[:, pl.ds(first, count), H + 1] = jnp.zeros((3, count, W, C), BF16)

        if count < F:

            @pl.when(t == edge)
            def _():
                for f in range(count):
                    for dw in range(3):
                        taps[dw, first + f] = jnp.zeros((H + 2, W, C), BF16)

    def convolve(f, weights, back):
        left = jnp.concatenate(
            [
                taps[dw, pl.ds(f + dt, 2), pl.ds(dh, H)].reshape(2 * H * W, C)
                for dt, dh, dw in TAPS
            ],
            axis=1,
        )
        if back:
            right = jnp.concatenate([weights[26 - n] for n in range(27)], axis=1)
            return lax.dot_general(left, right, (((1,), (1,)), ((), ())), preferred_element_type=F32)
        return jnp.dot(left, weights[...].reshape(27 * C, C), preferred_element_type=F32)

    def row_of(ref, i):
        return ref[pl.ds(i, 1), :]

    def sums(x):
        return jnp.sum(x.reshape(-1, 8, C), axis=0)

    def norm_grad(values, d, mean, inverse, gain, offset):
        normed = (values - mean) * inverse
        pre = normed * gain + offset
        s = sigmoid(pre)
        e = d * s * (1.0 + pre * (1.0 - s)) * gain
        return e, sums(e), sums(e * normed)

    for load in loads[4:]:
        load.wait()
    vectors = [ref[...].reshape(1, C) for ref in (bias1, gain1, offset1, gain2, offset2)]
    bias1, gain1, offset1, gain2, offset2 = vectors

    loads[0].wait()

    def first_sums(f, carry):
        x = actf[f + 2, pl.ds(1, H)].astype(F32).reshape(H * W, C)
        put_stage(f * H * W, x)
        part[0, f] = sums(x)
        part[1, f] = sums(x * x)
        return carry

    lax.fori_loop(0, F, first_sums, 0)
    mine[0] = packed_sums()
    pl.semaphore_wait(barrier, len(everyone))
    plane_start(0)
    past = rim_copies(0, actf, 2, 0, 1)
    start_all(past[0], past[1][1:])
    pack_rims(0)
    start_all(past[2], past[3])
    loads[1].wait()
    fill_stage(cotf)
    pack_rims(1)
    line_start(0, plane_end(0))
    start_all(past[1][:1])
    future = rim_copies(1, cotf, 0, 4, -1)
    start_all(future[0], future[2], future[1], future[3])
    stat1[...] = first_end()

    def activate(f, x):
        shape = (1,) * (x.ndim - 1) + (C,)
        mean = row_of(stat1, f).reshape(shape)
        inverse = row_of(stat1, f + 8).reshape(shape)
        u = (x - mean) * inverse * gain1.reshape(shape) + offset1.reshape(shape)
        return u * sigmoid(u)

    await_rims(past[0], past[2])
    side_columns((0,), 2, F, 1, activate)
    active_rows = lambda f, h: activate(f, actf[f, pl.ds(h, 6)].astype(F32))
    build(active_rows, 2, F, 0)
    loads[2].wait()

    def first_layer(i, carry):
        @pl.when(i == 1)
        def _():
            await_rims(past[1], past[3])
            side_columns((0,), 0, 2, 1, activate)
            build(active_rows, 0, 2, 0)

        f = 2 - 2 * i
        hidden = convolve(f, w1, False)
        x = actf[pl.ds(f + 2, 2), pl.ds(1, H)].astype(F32).reshape(2 * H * W, C)
        y = (x + hidden + bias1).astype(BF16)
        layf[pl.ds(f, 2), pl.ds(1, H)] = y.reshape(2, H, W, C)
        y = y.astype(F32)
        for j in range(2):
            z = y[j * H * W : (j + 1) * H * W]
            part[0, f + j] = sums(z)
            part[1, f + j] = sums(z * z)
        return carry

    lax.fori_loop(0, F // 2, first_layer, 0)
    chip_start(1, packed_sums(), True)
    layer_rims = rim_copies(2, layf, 0, 4, -1)
    start_all(layer_rims[1], layer_rims[0])
    fill_stage(layf)
    pack_rims(2)
    start_all(layer_rims[2], layer_rims[3])

    await_rims(future[0], future[2])
    loads[3].wait()
    same = lambda f, x: x
    side_columns((1,), 0, F, -1, same)
    cot_rows = lambda f, h: cotf[f, pl.ds(h, 6)].astype(F32)
    build(cot_rows, 0, F, tms - 1)

    def second_grad(i, carry):
        @pl.when(i == 1)
        def _():
            await_rims(future[1], future[3])
            side_columns((1,), 4, 2, -1, same)
            build(cot_rows, 4, 2, tms - 1)

        f = 2 * i
        grad[pl.ds(f, 2)] = convolve(f, w2, True).reshape(2, H, W, C)
        return carry

    lax.fori_loop(0, F // 2, second_grad, 0)
    stat2[...] = forward_end(1, 1)

    def second_norm(f, carry):
        mean, inverse = row_of(stat2, f), row_of(stat2, f + 8)
        a = b = jnp.zeros((8, C), F32)
        for h in range(0, H, 8):
            v = layf[f, pl.ds(h + 1, 8)].astype(F32).reshape(8 * W, C)
            d = grad[f, pl.ds(h, 8)].reshape(8 * W, C)
            e, da, db = norm_grad(v, d, mean, inverse, gain2, offset2)
            x = cotf[f, pl.ds(h + 1, 8)].astype(F32).reshape(8 * W, C) + inverse * e
            xwide[f, pl.ds(h + 1, 8)] = x.reshape(8, W, C)
            xf[f, pl.ds(h + 1, 8)] = x.astype(BF16).reshape(8, W, C)
            a, b = a + da, b + db
        part[0, f] = a
        part[1, f] = b
        return carry

    lax.fori_loop(0, 2, second_norm, 0)
    x_rims = rim_copies(3, xf, 0, 4, -1)
    start_all(x_rims[1][1:])
    lax.fori_loop(2, F, second_norm, 0)
    chip_start(2, backward_terms(packed_sums(), 1), False)
    start_all(x_rims[1][:1], x_rims[0])
    fill_stage(xf)
    pack_rims(3)
    start_all(x_rims[2], x_rims[3])
    await_rims(layer_rims[0], layer_rims[2], x_rims[0], x_rims[2])

    def widen_rows(f, carry):
        for h in (0, H + 1):
            xwide[f, h] = xf[f, h].astype(F32)
        return carry

    lax.fori_loop(0, F, widen_rows, 0)
    rest2[...] = backward_end(2)

    def settle(f, x, v):
        shape = (1,) * (x.ndim - 1) + (C,)
        r1 = row_of(rest2, f).reshape(shape)
        r2 = row_of(rest2, f + 8).reshape(shape)
        return x + (r1 + 2.0 * v * r2)

    def middle_rows(x):
        def get(f, h):
            g = settle(f, x[f, pl.ds(h, 6)].astype(F32), layf[f, pl.ds(h, 6)].astype(F32)).astype(BF16)
            gmf[f, pl.ds(h, 6)] = g
            return g.astype(F32)

        return get

    side_columns((3, 2), 0, F, -1, settle)
    build(middle_rows(xwide), 0, F, tms - 1)

    def first_grad(i, carry):
        @pl.when(i == 1)
        def _():
            await_rims(layer_rims[1], layer_rims[3], x_rims[1], x_rims[3])
            side_columns((3, 2), 4, 2, -1, settle)
            build(middle_rows(xf), 4, 2, tms - 1)

        both = convolve(2 * i, w1, True)
        for j in range(2):
            f = 2 * i + j
            mean, inverse = row_of(stat1, f + 2), row_of(stat1, f + 10)
            a = b = jnp.zeros((8, C), F32)
            for h in range(0, H, 8):
                v = actf[f + 2, pl.ds(h + 1, 8)].astype(F32).reshape(8 * W, C)
                d = both[(j * H + h) * W : (j * H + h + 8) * W]
                e, da, db = norm_grad(v, d, mean, inverse, gain1, offset1)
                x = gmf[f, pl.ds(h + 1, 8)].astype(F32).reshape(8 * W, C) + inverse * e
                grad[f, pl.ds(h, 8)] = x.reshape(8, W, C)
                a, b = a + da, b + db
            part[0, f] = a
            part[1, f] = b
        return carry

    lax.fori_loop(0, F // 2, first_grad, 0)
    chip_start(3, backward_terms(packed_sums(), 0), False)
    rest1[...] = backward_end(3)

    def finish(f, carry):
        r1, r2 = row_of(rest1, f), row_of(rest1, f + 8)
        for h in range(0, H, 8):
            v = actf[f + 2, pl.ds(h + 1, 8)].astype(F32).reshape(8 * W, C)
            y = grad[f, pl.ds(h, 8)].reshape(8 * W, C) + (r1 + 2.0 * v * r2)
            out_ref[f, pl.ds(h, 8)] = y.astype(BF16).reshape(8, W, C)
        return carry

    lax.fori_loop(0, F, finish, 0)

    for group in past + future + layer_rims + x_rims:
        for copy in group:
            copy.wait_send()
    await_all(plane_in.at[0], plane_send.at[0])
    await_all(line_in.at[0], line_send.at[0])
    for k in range(1, 4):
        await_all(near_in.at[k], near_send.at[k])
        for a in steps:

            @pl.when(goes(a, k == 1))
            def _(a=a, k=k):
                await_all(far_in.at[k, a - 1], far_send.at[k, a - 1])


def solution(mesh):
    sizes = tuple(mesh.shape[a] for a in AXES)
    n_plane, n_line = sizes[1] * sizes[2] - 1, sizes[0] - 1
    n_chips = sizes[1] * sizes[2] // 2
    rims = 18
    full = (F + 2, H + 2, W, C)

    def step(act, cot, w1, b1, g1, o1, w2, g2, o2):
        hbm = pl.BlockSpec(memory_space=pltpu.HBM)
        operands = (act, cot, w1.reshape(27, C, C), w2.reshape(27, C, C), b1, g1, o1, g2, o2)
        operands = [pltpu.with_memory_space_constraint(x, pltpu.HBM) for x in operands]
        vmem = pl.BlockSpec(memory_space=pltpu.VMEM)
        return pl.pallas_call(
            functools.partial(kernel, sizes),
            name="vae_grad",
            out_shape=pltpu.VMEM((F, H, W, C), BF16),
            in_specs=[hbm] * 9,
            out_specs=vmem,
            scratch_shapes=[
                pltpu.VMEM(full, BF16),
                pltpu.VMEM(full, BF16),
                pltpu.VMEM(full, BF16),
                pltpu.VMEM((27, C, C), BF16),
                pltpu.VMEM((27, C, C), BF16),
                pltpu.VMEM((C,), F32),
                pltpu.VMEM((C,), F32),
                pltpu.VMEM((C,), F32),
                pltpu.VMEM((C,), F32),
                pltpu.VMEM((C,), F32),
                pltpu.VMEM((3,) + full, BF16),
                pltpu.VMEM((F, H, W, C), F32),
                pltpu.VMEM(full, BF16),
                pltpu.VMEM(full, BF16),
                pltpu.VMEM(full, F32),
                pltpu.VMEM((2, F * H * W, 128), F32),
                pltpu.VMEM((4, 2, F, H, C), BF16),
                pltpu.VMEM((4, 2, 2, F, C), F32),
                pltpu.VMEM((4, 2, F + 2, H, C), BF16),
                pltpu.VMEM((4, 2, 2, 2, F, C), F32),
                pltpu.VMEM((2, F + 2, 24, C), F32),
                pltpu.VMEM((2, F, 8, C), F32),
                pltpu.VMEM((C, 128), BF16),
                pltpu.VMEM((128, C), BF16),
                pltpu.VMEM((16, C), F32),
                pltpu.VMEM((16, C), F32),
                pltpu.VMEM((16, C), F32),
                pltpu.VMEM((16, C), F32),
                pltpu.VMEM((2, 2, 128), F32),
                pltpu.VMEM((4, 2, 128), F32),
                pltpu.VMEM((4, 2, 128), F32),
                pltpu.VMEM((1, n_plane, 2, 128), F32),
                pltpu.VMEM((1, n_line, 2, 128), F32),
                pltpu.VMEM((4, 2, 128), F32),
                pltpu.VMEM((4, 1, 128), F32),
                pltpu.VMEM((4, 2, 128), F32),
                pltpu.VMEM((4, n_chips - 1, 2, 128), F32),
                pltpu.VMEM((4, n_line, n_chips, 1, 128), F32),
                pltpu.VMEM((n_line, 1, 128), F32),
                pltpu.SemaphoreType.DMA((9,)),
                pltpu.SemaphoreType.DMA((4, rims)),
                pltpu.SemaphoreType.DMA((4, rims)),
                *[pltpu.SemaphoreType.DMA((4,))] * 8,
                *[pltpu.SemaphoreType.DMA((4, n_line))] * 2,
            ],
            compiler_params=pltpu.CompilerParams(
                collective_id=0, has_side_effects=True, vmem_limit_bytes=62 << 20
            ),
        )(*operands)

    tile = P(*AXES, None)
    return jax.shard_map(
        step,
        mesh=mesh,
        in_specs=(tile, tile) + (P(),) * 7,
        out_specs=tile,
        check_vma=False,
    )
```
